32 devices in a mesh: comp: 8 (over z, y), seq: 4 (over x, core).
Axes of the slice: x: 2, y: 2, z: 4, core: 2. Of those that a mesh axis runs over, the one named last changes fastest.
Arguments:
- queries: bfloat16 [8, 512, 4096], P('comp', 'seq'), may hold values from -24 to 24
- keys: bfloat16 [8, 512, 4096], P('comp', 'seq'), may hold values from -24 to 24
- values: bfloat16 [8, 512, 4096], P('comp', 'seq'), may hold values from -6 to 6
- latent: float32 [64, 512], P('comp', 'seq'), may hold values from -6 to 6
- prev_denoised: float32 [64, 512], P('comp', 'seq'), may hold values from -6 to 6
- head_weight: bfloat16 [4096, 64], P('seq'), may hold values from -0.09375 to 0.09375
Outputs:
- hidden: bfloat16 [8, 512, 4096], P('comp', 'seq')
- new_latent: float32 [64, 512], P('comp', 'seq')
- denoised: float32 [64, 512], P('comp', 'seq')
The draws below stay inside these ranges and needn't reach their ends.
All inputs are finite; a program needn't handle non-finite values.
Results may differ from the reference program's by a relative error of at most 0.008.
Values may be sent and summed in bfloat16 or wider, within the bound.
A program may use at most 64 MiB of HBM per device.

```python
import math
import jax
import jax.numpy as jnp
from jax import lax

HEADS = 32
HD = 128
LATENT = 64
TOKENS = 512
COMP = 8
WIDTH = 4096


def draw_queries(key, part):
    key = jax.random.fold_in(key, 1)
    result = jnp.clip(jax.random.normal(key, (COMP, TOKENS, WIDTH), jnp.float32), -4.0, 4.0)
    return result.astype(jnp.bfloat16)


def draw_keys(key, part):
    key = jax.random.fold_in(key, 2)
    result = jnp.clip(jax.random.normal(key, (COMP, TOKENS, WIDTH), jnp.float32), -4.0, 4.0)
    return result.astype(jnp.bfloat16)


def levels(own_key, extent, shards, low, top_value):
    def one(position, parts):
        draws = jax.random.uniform(jax.random.fold_in(jax.random.fold_in(own_key, 6), position), (parts,), jnp.float32, low / len(shards), top_value / len(shards))
        return jnp.repeat(jnp.exp(draws), extent[position] // parts).reshape((-1,) + (1,) * (len(extent) - position - 1))

    factor_of = one(*shards[0])
    for cut in shards[1:]:
        factor_of = factor_of * one(*cut)
    return factor_of


def centred(own_key, extent, spread, most, split=(), dtype=jnp.bfloat16):
    drawn = jax.random.normal(own_key, extent, jnp.float32) * spread
    if len(split) > 0:
        drawn = levels(own_key, extent, split, -0.22, 0.18) * drawn
    return jnp.clip(drawn, min=-most, max=most).astype(dtype)


def setup_inputs(seed: int = 0) -> dict:
    streams_of = jax.random.split(jax.random.key(seed), 7)
    queries = draw_queries(jax.random.fold_in(streams_of[6], 71), 0)
    keys = draw_keys(jax.random.fold_in(streams_of[6], 71), 0)
    values = centred(streams_of[2], (COMP, TOKENS, WIDTH), 1.0, 6.0, ((0, 8), (1, 4)))
    latent = centred(streams_of[3], (LATENT, TOKENS), 1.0, 6.0, ((0, 8), (1, 4)), jnp.float32)
    prev_denoised = centred(streams_of[4], (LATENT, TOKENS), 1.0, 6.0, ((0, 8), (1, 4)), jnp.float32)
    head_weight = centred(streams_of[5], (WIDTH, LATENT), WIDTH ** -0.5, 0.09375, ((0, 4),))
    return {"queries": queries, "keys": keys, "values": values, "latent": latent, "prev_denoised": prev_denoised, "head_weight": head_weight}


alpha_now = 0.6
sigma_now = 0.8
alpha_next = 0.8
sigma_next = 0.6
step_before = 0.4

def head_attention(query_head, key_head, value_head):
    length = query_head.shape[0]
    block = math.gcd(length, 512)
    scale = query_head.shape[1] ** (-0.5)

    def one_block(query_block):
        scores = jnp.dot(query_block, key_head.T, preferred_element_type=jnp.float32) * scale
        highest = lax.optimization_barrier(jnp.max(scores, axis=1, keepdims=True))
        weights = jnp.exp(scores - highest)
        totals = lax.optimization_barrier(jnp.sum(weights, axis=1, keepdims=True))
        probs = (weights / totals).astype(jnp.bfloat16)
        return jnp.dot(probs, value_head, preferred_element_type=jnp.float32).astype(jnp.bfloat16)
    blocks = query_head.reshape(length // block, block, query_head.shape[1])
    return lax.map(one_block, blocks).reshape(length, query_head.shape[1])

def component_layer(operands):
    query_all, key_all, value_all = operands
    length = query_all.shape[0]

    def split_heads(array):
        return array.reshape(length, HEADS, HD).transpose(1, 0, 2)
    outputs = lax.map(lambda trio: head_attention(trio[0], trio[1], trio[2]), (split_heads(query_all), split_heads(key_all), split_heads(value_all)))
    return outputs.transpose(1, 0, 2).reshape(length, HEADS * HD)

def reference(queries, keys, values, latent, prev_denoised, head_weight):
    hidden = lax.map(component_layer, (queries, keys, values))
    last_layer = hidden[COMP - 1]
    squares = lax.optimization_barrier(jnp.mean(jnp.square(last_layer.astype(jnp.float32)), axis=1))
    norm_root = jnp.sqrt(squares + 1e-06)
    projected = jnp.dot(last_layer, head_weight, preferred_element_type=jnp.float32)
    noise = (projected / norm_root[:, None]).T
    denoised = (latent - sigma_now * noise) / alpha_now
    step_now = math.log(alpha_next / sigma_next) - math.log(alpha_now / sigma_now)
    ratio = step_before / step_now
    blend = (1.0 + 0.5 / ratio) * denoised - 0.5 / ratio * prev_denoised
    new_latent = sigma_next / sigma_now * latent - alpha_next * (math.exp(-step_now) - 1.0) * blend
    return (hidden, new_latent, denoised)
```

```python
import functools
import math

import jax
import jax.numpy as jnp
from jax import lax
from jax.experimental import pallas as pl
from jax.experimental.pallas import tpu as pltpu
from jax.sharding import PartitionSpec as P

HD = 128
CHUNKS = 8
MESH = pl.DeviceIdType.MESH

alpha_now = 0.6
sigma_now = 0.8
alpha_next = 0.8
sigma_next = 0.6
step_before = 0.4


def kernel(
    n, comps, own, q_hbm, k_hbm, v_hbm, w_hbm, hid_hbm, noise_ref,
    kbuf, vbuf, qbuf, obuf, wbuf, acc, sq, nsend, nrecv,
    k_send, k_recv, v_send, v_recv, q_send, q_recv, q_local,
    o_send, o_recv, o_local, w_send, w_recv, n_send, n_recv,
):
    tokens, width = hid_hbm.shape
    half = width // 2
    chips = n // 2
    cw = half // CHUNKS
    rows_w = width // n
    pad = nsend.shape[2] - 8
    comp = lax.axis_index("comp")
    me = lax.axis_index("seq")
    chip, core = me // 2, me % 2
    mate = chip * 2 + 1 - core
    last = comp == comps - 1

    def peer(d_chip, d_core):
        return lax.rem(chip + d_chip, chips) * 2 + lax.rem(core + d_core, 2)

    barrier = pltpu.get_barrier_semaphore()
    others = [(dx, dc) for dx in range(chips) for dc in range(2) if (dx, dc) != (0, 0)]
    for dx, dc in others:
        pl.semaphore_signal(barrier, inc=1, device_id=(comp, peer(dx, dc)), device_id_type=MESH)

    @pl.when(jnp.logical_not(last))
    def _():
        for target in (me, mate):
            pl.semaphore_signal(
                barrier, inc=1, device_id=(comps - 1, target), device_id_type=MESH
            )
        pl.semaphore_wait(barrier, n - 1)

    @pl.when(last)
    def _():
        pl.semaphore_wait(barrier, n - 1 + 2 * (comps - 1))

    def columns(side, j):
        return pl.ds(pl.multiple_of(side * half + j * cw, cw), cw)

    def kept(j):
        return pl.ds(pl.multiple_of(j * cw, cw), cw)

    def remote(src, dst, send, recv, target):
        return pltpu.make_async_remote_copy(
            src_ref=src, dst_ref=dst, send_sem=send, recv_sem=recv,
            device_id=(comp, target), device_id_type=MESH,
        )

    def kv_copies(dx, dc, j):
        target = peer(dx, dc)
        side = lax.rem(core + dc, 2)
        slot = ((chips - dx) % chips) * 2 + dc
        return [
            remote(src.at[0, :, columns(side, j)], buf.at[slot, :, kept(j)],
                   send.at[slot, j], recv.at[slot, j], target)
            for src, buf, send, recv in (
                (k_hbm, kbuf, k_send, k_recv), (v_hbm, vbuf, v_send, v_recv))
        ]

    def q_copy(j):
        return remote(q_hbm.at[0, :, columns(1 - core, j)], qbuf.at[1, :, kept(j)],
                      q_send.at[j], q_recv.at[j], mate)

    def local_copies(j):
        mine = columns(core, j)
        return [
            pltpu.make_async_copy(q_hbm.at[0, :, mine], qbuf.at[0, :, kept(j)], q_local.at[j]),
            pltpu.make_async_copy(k_hbm.at[0, :, mine], kbuf.at[0, :, kept(j)], k_recv.at[0, j]),
            pltpu.make_async_copy(v_hbm.at[0, :, mine], vbuf.at[0, :, kept(j)], v_recv.at[0, j]),
        ]

    def o_copies(j):
        mine = columns(core, j)
        return [
            pltpu.make_async_copy(obuf.at[0, :, kept(j)], hid_hbm.at[:, mine], o_local.at[j]),
            remote(obuf.at[1, :, kept(j)], hid_hbm.at[:, mine], o_send.at[j], o_recv.at[j], mate),
        ]

    w_side = me // chips
    w_slot = lax.rem(me, chips)

    def w_copy(x):
        return remote(w_hbm, wbuf.at[w_slot], w_send.at[x], w_recv.at[w_slot], x * 2 + w_side)

    @pl.when(last)
    def _():
        for x in range(chips):
            @pl.when(x * 2 + w_side != me)
            def _():
                w_copy(x).start()

            @pl.when(x * 2 + w_side == me)
            def _():
                pltpu.make_async_copy(w_hbm, wbuf.at[w_slot], w_recv.at[w_slot]).start()

        acc[...] = jnp.zeros_like(acc)
        sq[...] = jnp.zeros_like(sq)

    def start_chunk(j, carry):
        for dx in range(1, chips):
            for dc in range(2):
                for copy in kv_copies(dx, dc, j):
                    copy.start()
        for copy in kv_copies(0, 1, j):
            copy.start()
        q_copy(j).start()
        for copy in local_copies(j):
            copy.start()
        return carry

    lax.fori_loop(0, CHUNKS, start_chunk, 0)

    @pl.when(last)
    def _():
        for x in range(chips):
            pltpu.make_async_copy(w_hbm, wbuf.at[x], w_recv.at[x]).wait()

    factor = HD ** (-0.5) * math.log2(math.e)

    def attend(j, carry):
        for copy in local_copies(j):
            copy.wait()
        q_copy(j).wait_recv()
        for dx, dc in others:
            for copy in kv_copies(dx, dc, j):
                copy.wait_recv()
        for h in range(cw // HD):
            cols = pl.ds(pl.multiple_of(j * cw + h * HD, HD), HD)
            query = qbuf[:, :, cols].reshape(2 * tokens, HD)
            key = kbuf[:, :, cols].reshape(n * tokens, HD)
            value = vbuf[:, :, cols].reshape(n * tokens, HD)
            scores = lax.dot_general(
                query, key, (((1,), (1,)), ((), ())), preferred_element_type=jnp.float32
            )
            highest = jnp.max(scores, axis=1, keepdims=True)
            weights = jnp.exp2((scores - highest) * factor)
            totals = jnp.sum(weights, axis=1, keepdims=True)
            out = jnp.dot(weights.astype(jnp.bfloat16), value, preferred_element_type=jnp.float32)
            out = (out / totals).astype(jnp.bfloat16)
            obuf[:, :, cols] = out.reshape(2, tokens, HD)
        for copy in o_copies(j):
            copy.start()

        @pl.when(last)
        def _():
            part = obuf[:, :, kept(j)].reshape(2 * tokens, cw)
            rows = wbuf.reshape(half, wbuf.shape[2])[kept(j), :]
            acc[...] += jnp.dot(part, rows, preferred_element_type=jnp.float32)
            wide = part.astype(jnp.float32)
            sq[...] += jnp.sum(wide * wide, axis=1, keepdims=True)

        return carry

    lax.fori_loop(0, CHUNKS, attend, 0)

    def noise_copy(c, side):
        return pltpu.make_async_remote_copy(
            src_ref=nsend.at[c, side], dst_ref=nrecv.at[side],
            send_sem=n_send.at[c, side], recv_sem=n_recv.at[side],
            device_id=(c, me if side == 0 else mate), device_id_type=MESH,
        )

    def noise_self():
        return pltpu.make_async_copy(nsend.at[comps - 1, 0], nrecv.at[0], n_recv.at[0])

    @pl.when(last)
    def _():
        both = jnp.concatenate([acc[...], jnp.broadcast_to(sq[...], acc.shape)], axis=1).T
        channels = acc.shape[1]
        for c in range(comps):
            for side in range(2):
                toks = slice(side * tokens, (side + 1) * tokens)
                nsend[c, side, 0:own, :] = both[c * own:(c + 1) * own, toks]
                nsend[c, side, pad:pad + 8, :] = both[channels:channels + 8, toks]
        for c in range(comps):
            for side in range(2):
                if (c, side) == (comps - 1, 0):
                    noise_self().start()
                else:
                    noise_copy(c, side).start()

    def drain(j, carry):
        for dx, dc in others:
            for copy in kv_copies(dx, dc, j):
                copy.wait_send()
        q_copy(j).wait_send()
        local, back = o_copies(j)
        local.wait()
        back.wait()
        return carry

    lax.fori_loop(0, CHUNKS, drain, 0)

    @pl.when(last)
    def _():
        for x in range(chips):
            @pl.when(x * 2 + w_side != me)
            def _():
                w_copy(x).wait_send()
        for c in range(comps):
            for side in range(2):
                if (c, side) != (comps - 1, 0):
                    noise_copy(c, side).wait_send()

    for side in range(2):
        pltpu.make_async_copy(nsend.at[0, side], nrecv.at[side], n_recv.at[side]).wait()
    total = nrecv[0] + nrecv[1]
    root = jnp.sqrt(total[pad:pad + 1] / width + 1e-06)
    noise_ref[...] = total[0:own] / root


def on_device(queries, keys, values, latent, prev_denoised, head_weight):
    n = lax.axis_size("seq")
    comps = lax.axis_size("comp")
    _, tokens, width = queries.shape
    half = width // 2
    own = latent.shape[0]
    channels = head_weight.shape[1]
    pad = -(-own // 8) * 8
    bf16, f32 = jnp.bfloat16, jnp.float32
    dma = pltpu.SemaphoreType.DMA
    anywhere = pl.BlockSpec(memory_space=pl.ANY)
    hidden, noise_own = pl.pallas_call(
        functools.partial(kernel, n, comps, own),
        out_shape=(
            jax.ShapeDtypeStruct((tokens, width), bf16),
            jax.ShapeDtypeStruct((own, tokens), f32),
        ),
        in_specs=[anywhere] * 4,
        out_specs=(anywhere, pl.BlockSpec(memory_space=pltpu.VMEM)),
        scratch_shapes=[
            pltpu.VMEM((n, tokens, half), bf16),
            pltpu.VMEM((n, tokens, half), bf16),
            pltpu.VMEM((2, tokens, half), bf16),
            pltpu.VMEM((2, tokens, half), bf16),
            pltpu.VMEM((n // 2, width // n, channels), bf16),
            pltpu.VMEM((2 * tokens, channels), f32),
            pltpu.VMEM((2 * tokens, 1), f32),
            pltpu.VMEM((comps, 2, pad + 8, tokens), f32),
            pltpu.VMEM((2, pad + 8, tokens), f32),
            dma((n, CHUNKS)), dma((n, CHUNKS)), dma((n, CHUNKS)), dma((n, CHUNKS)),
            dma((CHUNKS,)), dma((CHUNKS,)), dma((CHUNKS,)),
            dma((CHUNKS,)), dma((CHUNKS,)), dma((CHUNKS,)),
            dma((n // 2,)), dma((n // 2,)),
            dma((comps, 2)), dma((2,)),
        ],
        compiler_params=pltpu.CompilerParams(
            collective_id=0, has_side_effects=True, vmem_limit_bytes=48 * 1024 * 1024
        ),
        name="attention_step",
    )(queries, keys, values, head_weight)
    denoised = (latent - sigma_now * noise_own) / alpha_now
    step_now = math.log(alpha_next / sigma_next) - math.log(alpha_now / sigma_now)
    ratio = step_before / step_now
    blend = (1.0 + 0.5 / ratio) * denoised - 0.5 / ratio * prev_denoised
    new_latent = sigma_next / sigma_now * latent - alpha_next * (math.exp(-step_now) - 1.0) * blend
    return (hidden[None], new_latent, denoised)


def solution(mesh):
    return jax.shard_map(
        on_device,
        mesh=mesh,
        in_specs=(
            P("comp", "seq", None),
            P("comp", "seq", None),
            P("comp", "seq", None),
            P("comp", "seq"),
            P("comp", "seq"),
            P("seq", None),
        ),
        out_specs=(P("comp", "seq", None), P("comp", "seq"), P("comp", "seq")),
        check_vma=False,
    )
```

```python
import functools
import math

import jax
import jax.numpy as jnp
from jax import lax
from jax.experimental import pallas as pl
from jax.experimental.pallas import tpu as pltpu
from jax.sharding import PartitionSpec as P

HD = 128
CHUNKS = 8
WINDOW = 3
MESH = pl.DeviceIdType.MESH

alpha_now = 0.6
sigma_now = 0.8
alpha_next = 0.8
sigma_next = 0.6
step_before = 0.4


def kernel(
    n, comps, own, q_hbm, k_hbm, v_hbm, w_hbm, hid_hbm, noise_ref,
    kbuf, vbuf, qbuf, obuf, wbuf, acc, sq, nsend, nrecv,
    k_send, k_recv, v_send, v_recv, q_send, q_recv, q_local,
    o_send, o_recv, o_local, w_send, w_recv, n_send, n_recv,
):
    tokens, width = hid_hbm.shape
    half = width // 2
    chips = n // 2
    cw = half // CHUNKS
    rows_w = width // n
    pad = nsend.shape[2] - 8
    comp = lax.axis_index("comp")
    me = lax.axis_index("seq")
    chip, core = me // 2, me % 2
    mate = chip * 2 + 1 - core
    last = comp == comps - 1

    def peer(d_chip, d_core):
        return lax.rem(chip + d_chip, chips) * 2 + lax.rem(core + d_core, 2)

    barrier = pltpu.get_barrier_semaphore()
    others = [(dx, dc) for dx in range(chips) for dc in range(2) if (dx, dc) != (0, 0)]
    for dx, dc in others:
        pl.semaphore_signal(barrier, inc=1, device_id=(comp, peer(dx, dc)), device_id_type=MESH)

    @pl.when(jnp.logical_not(last))
    def _():
        for target in (me, mate):
            pl.semaphore_signal(
                barrier, inc=1, device_id=(comps - 1, target), device_id_type=MESH
            )
        pl.semaphore_wait(barrier, n - 1)

    @pl.when(last)
    def _():
        pl.semaphore_wait(barrier, n - 1 + 2 * (comps - 1))

    def columns(side, j):
        return pl.ds(pl.multiple_of(side * half + j * cw, cw), cw)

    def kept(j):
        return pl.ds(pl.multiple_of(j * cw, cw), cw)

    def remote(src, dst, send, recv, target):
        return pltpu.make_async_remote_copy(
            src_ref=src, dst_ref=dst, send_sem=send, recv_sem=recv,
            device_id=(comp, target), device_id_type=MESH,
        )

    def kv_copies(dx, dc, j):
        target = peer(dx, dc)
        side = lax.rem(core + dc, 2)
        slot = ((chips - dx) % chips) * 2 + dc
        return [
            remote(src.at[0, :, columns(side, j)], buf.at[slot, :, kept(j)],
                   send.at[slot, j], recv.at[slot, j], target)
            for src, buf, send, recv in (
                (k_hbm, kbuf, k_send, k_recv), (v_hbm, vbuf, v_send, v_recv))
        ]

    def q_copy(j):
        return remote(q_hbm.at[0, :, columns(1 - core, j)], qbuf.at[1, :, kept(j)],
                      q_send.at[j], q_recv.at[j], mate)

    def local_copies(j):
        mine = columns(core, j)
        return [
            pltpu.make_async_copy(q_hbm.at[0, :, mine], qbuf.at[0, :, kept(j)], q_local.at[j]),
            pltpu.make_async_copy(k_hbm.at[0, :, mine], kbuf.at[0, :, kept(j)], k_recv.at[0, j]),
            pltpu.make_async_copy(v_hbm.at[0, :, mine], vbuf.at[0, :, kept(j)], v_recv.at[0, j]),
        ]

    def o_copies(j):
        mine = columns(core, j)
        return [
            pltpu.make_async_copy(obuf.at[0, :, kept(j)], hid_hbm.at[:, mine], o_local.at[j]),
            remote(obuf.at[1, :, kept(j)], hid_hbm.at[:, mine], o_send.at[j], o_recv.at[j], mate),
        ]

    w_side = me // chips
    w_slot = lax.rem(me, chips)

    def w_copy(x):
        return remote(w_hbm, wbuf.at[w_slot], w_send.at[x], w_recv.at[w_slot], x * 2 + w_side)

    @pl.when(last)
    def _():
        for x in range(chips):
            @pl.when(x * 2 + w_side != me)
            def _():
                w_copy(x).start()

            @pl.when(x * 2 + w_side == me)
            def _():
                pltpu.make_async_copy(w_hbm, wbuf.at[w_slot], w_recv.at[w_slot]).start()

        acc[...] = jnp.zeros_like(acc)
        sq[...] = jnp.zeros_like(sq)

    def start_chunk(j, carry):
        for dx in range(1, chips):
            for dc in range(2):
                for copy in kv_copies(dx, dc, j):
                    copy.start()
        for copy in kv_copies(0, 1, j):
            copy.start()
        q_copy(j).start()
        for copy in local_copies(j):
            copy.start()
        return carry

    lax.fori_loop(0, WINDOW, start_chunk, 0)

    @pl.when(last)
    def _():
        for x in range(chips):
            pltpu.make_async_copy(w_hbm, wbuf.at[x], w_recv.at[x]).wait()

    factor = HD ** (-0.5) * math.log2(math.e)

    def attend(j, carry):
        for copy in local_copies(j):
            copy.wait()
        q_copy(j).wait_recv()
        for dx, dc in others:
            for copy in kv_copies(dx, dc, j):
                copy.wait_recv()

        @pl.when(j + WINDOW < CHUNKS)
        def _():
            start_chunk(j + WINDOW, 0)

        for h in range(cw // HD):
            cols = pl.ds(pl.multiple_of(j * cw + h * HD, HD), HD)
            query = qbuf[:, :, cols].reshape(2 * tokens, HD)
            key = kbuf[:, :, cols].reshape(n * tokens, HD)
            value = vbuf[:, :, cols].reshape(n * tokens, HD)
            scores = lax.dot_general(
                query, key, (((1,), (1,)), ((), ())), preferred_element_type=jnp.float32
            )
            highest = jnp.max(scores, axis=1, keepdims=True)
            weights = jnp.exp2((scores - highest) * factor)
            totals = jnp.sum(weights, axis=1, keepdims=True)
            out = jnp.dot(weights.astype(jnp.bfloat16), value, preferred_element_type=jnp.float32)
            out = (out / totals).astype(jnp.bfloat16)
            obuf[:, :, cols] = out.reshape(2, tokens, HD)
        for copy in o_copies(j):
            copy.start()

        @pl.when(last)
        def _():
            part = obuf[:, :, kept(j)].reshape(2 * tokens, cw)
            first = j * cw
            rows = wbuf[first // rows_w, :, pl.ds(pl.multiple_of(first % rows_w, cw), cw)]
            acc[...] += lax.dot_general(
                part, rows, (((1,), (1,)), ((), ())), preferred_element_type=jnp.float32
            )
            wide = part.astype(jnp.float32)
            sq[...] += jnp.sum(wide * wide, axis=1, keepdims=True)

        return carry

    lax.fori_loop(0, CHUNKS, attend, 0)

    def noise_copy(c, side):
        return pltpu.make_async_remote_copy(
            src_ref=nsend.at[c, side], dst_ref=nrecv.at[side],
            send_sem=n_send.at[c, side], recv_sem=n_recv.at[side],
            device_id=(c, me if side == 0 else mate), device_id_type=MESH,
        )

    def noise_self():
        return pltpu.make_async_copy(nsend.at[comps - 1, 0], nrecv.at[0], n_recv.at[0])

    @pl.when(last)
    def _():
        both = jnp.concatenate([acc[...], jnp.broadcast_to(sq[...], acc.shape)], axis=1).T
        channels = acc.shape[1]
        for c in range(comps):
            for side in range(2):
                toks = slice(side * tokens, (side + 1) * tokens)
                nsend[c, side, 0:own, :] = both[c * own:(c + 1) * own, toks]
                nsend[c, side, pad:pad + 8, :] = both[channels:channels + 8, toks]
        for c in range(comps):
            for side in range(2):
                if (c, side) == (comps - 1, 0):
                    noise_self().start()
                else:
                    noise_copy(c, side).start()

    def drain(j, carry):
        for dx, dc in others:
            for copy in kv_copies(dx, dc, j):
                copy.wait_send()
        q_copy(j).wait_send()
        local, back = o_copies(j)
        local.wait()
        back.wait()
        return carry

    lax.fori_loop(0, CHUNKS, drain, 0)

    @pl.when(last)
    def _():
        for x in range(chips):
            @pl.when(x * 2 + w_side != me)
            def _():
                w_copy(x).wait_send()
        for c in range(comps):
            for side in range(2):
                if (c, side) != (comps - 1, 0):
                    noise_copy(c, side).wait_send()

    for side in range(2):
        pltpu.make_async_copy(nsend.at[0, side], nrecv.at[side], n_recv.at[side]).wait()
    total = nrecv[0] + nrecv[1]
    root = jnp.sqrt(total[pad:pad + 1] / width + 1e-06)
    noise_ref[...] = total[0:own] / root


def on_device(queries, keys, values, latent, prev_denoised, head_weight):
    n = lax.axis_size("seq")
    comps = lax.axis_size("comp")
    _, tokens, width = queries.shape
    half = width // 2
    own = latent.shape[0]
    channels = head_weight.shape[1]
    pad = -(-own // 8) * 8
    bf16, f32 = jnp.bfloat16, jnp.float32
    dma = pltpu.SemaphoreType.DMA
    anywhere = pl.BlockSpec(memory_space=pl.ANY)
    hidden, noise_own = pl.pallas_call(
        functools.partial(kernel, n, comps, own),
        out_shape=(
            jax.ShapeDtypeStruct((tokens, width), bf16),
            jax.ShapeDtypeStruct((own, tokens), f32),
        ),
        in_specs=[anywhere] * 4,
        out_specs=(anywhere, pl.BlockSpec(memory_space=pltpu.VMEM)),
        scratch_shapes=[
            pltpu.VMEM((n, tokens, half), bf16),
            pltpu.VMEM((n, tokens, half), bf16),
            pltpu.VMEM((2, tokens, half), bf16),
            pltpu.VMEM((2, tokens, half), bf16),
            pltpu.VMEM((n // 2, channels, width // n), bf16),
            pltpu.VMEM((2 * tokens, channels), f32),
            pltpu.VMEM((2 * tokens, 1), f32),
            pltpu.VMEM((comps, 2, pad + 8, tokens), f32),
            pltpu.VMEM((2, pad + 8, tokens), f32),
            dma((n, CHUNKS)), dma((n, CHUNKS)), dma((n, CHUNKS)), dma((n, CHUNKS)),
            dma((CHUNKS,)), dma((CHUNKS,)), dma((CHUNKS,)),
            dma((CHUNKS,)), dma((CHUNKS,)), dma((CHUNKS,)),
            dma((n // 2,)), dma((n // 2,)),
            dma((comps, 2)), dma((2,)),
        ],
        compiler_params=pltpu.CompilerParams(
            collective_id=0, has_side_effects=True, vmem_limit_bytes=60 * 1024 * 1024
        ),
        name="attention_step",
    )(queries, keys, values, head_weight.T)
    denoised = (latent - sigma_now * noise_own) / alpha_now
    step_now = math.log(alpha_next / sigma_next) - math.log(alpha_now / sigma_now)
    ratio = step_before / step_now
    blend = (1.0 + 0.5 / ratio) * denoised - 0.5 / ratio * prev_denoised
    new_latent = sigma_next / sigma_now * latent - alpha_next * (math.exp(-step_now) - 1.0) * blend
    return (hidden[None], new_latent, denoised)


def solution(mesh):
    return jax.shard_map(
        on_device,
        mesh=mesh,
        in_specs=(
            P("comp", "seq", None),
            P("comp", "seq", None),
            P("comp", "seq", None),
            P("comp", "seq"),
            P("comp", "seq"),
            P("seq", None),
        ),
        out_specs=(P("comp", "seq", None), P("comp", "seq"), P("comp", "seq")),
        check_vma=False,
    )
```

```python
import functools
import math

import jax
import jax.numpy as jnp
from jax import lax
from jax.experimental import pallas as pl
from jax.experimental.pallas import tpu as pltpu
from jax.sharding import PartitionSpec as P

HD = 128
CHUNKS = 8
WINDOW = 3
LATE = 5
MESH = pl.DeviceIdType.MESH

alpha_now = 0.6
sigma_now = 0.8
alpha_next = 0.8
sigma_next = 0.6
step_before = 0.4


def kernel(
    n, comps, own, q_hbm, k_hbm, v_hbm, w_hbm, hid_hbm, noise_ref,
    kbuf, vbuf, qbuf, obuf, wbuf, acc, sq, nsend, nrecv, relay_in, relay_mid, w_mid,
    k_send, k_recv, v_send, v_recv, q_send, q_recv, q_local,
    o_send, o_recv, o_local, w_send, w_recv, n_send, n_recv,
    in_send, in_recv, mid_send, mid_recv, back_send, piece_recv,
    wm_send, wm_recv, wb_send, w_piece, ready,
):
    tokens, width = hid_hbm.shape
    half = width // 2
    chips = n // 2
    cw = half // CHUNKS
    rows_w = width // n
    pad = nsend.shape[2] - 8
    comp = lax.axis_index("comp")
    me = lax.axis_index("seq")
    chip, core = me // 2, me % 2
    mate = chip * 2 + 1 - core
    last = comp == comps - 1

    def peer(d_chip, d_core):
        return lax.rem(chip + d_chip, chips) * 2 + lax.rem(core + d_core, 2)

    barrier = pltpu.get_barrier_semaphore()
    others = [(dx, dc) for dx in range(chips) for dc in range(2) if (dx, dc) != (0, 0)]
    for dx, dc in others:
        pl.semaphore_signal(barrier, inc=1, device_id=(comp, peer(dx, dc)), device_id_type=MESH)

    @pl.when(last)
    def _():
        for c in range(comps - 1):
            for target in (me, mate):
                pl.semaphore_signal(barrier, inc=1, device_id=(c, target), device_id_type=MESH)
        pl.semaphore_wait(barrier, n - 1)

    @pl.when(jnp.logical_not(last))
    def _():
        pl.semaphore_wait(barrier, n + 1)
        for target in (me, mate):
            pl.semaphore_signal(ready, inc=1, device_id=(comps - 1, target), device_id_type=MESH)

    pieces, piece_rows = piece_recv.shape[0], relay_in.shape[2]
    w_pieces, piece_cols = w_piece.shape[0], w_mid.shape[2]
    helper = jnp.logical_and(jnp.logical_not(last), comp >= comps - pieces)
    w_helper = jnp.logical_and(jnp.logical_not(last), comp >= comps - w_pieces)
    final = CHUNKS - 1
    far = [(dx, dc) for dx in range(1, chips) for dc in range(2)]
    far_slots = [((chips - dx) % chips) * 2 + dc for dx, dc in far]

    def columns(side, j):
        return pl.ds(pl.multiple_of(side * half + j * cw, cw), cw)

    def kept(j):
        return pl.ds(pl.multiple_of(j * cw, cw), cw)

    def remote(src, dst, send, recv, target, owner=comp):
        return pltpu.make_async_remote_copy(
            src_ref=src, dst_ref=dst, send_sem=send, recv_sem=recv,
            device_id=(owner, target), device_id_type=MESH,
        )

    def kv_copies(dx, dc, j):
        target = peer(dx, dc)
        side = lax.rem(core + dc, 2)
        slot = ((chips - dx) % chips) * 2 + dc
        return [
            remote(src.at[0, :, columns(side, j)], buf.at[slot, :, kept(j)],
                   send.at[slot, j], recv.at[slot, j], target)
            for src, buf, send, recv in (
                (k_hbm, kbuf, k_send, k_recv), (v_hbm, vbuf, v_send, v_recv))
        ]

    def q_copy(j):
        return remote(q_hbm.at[0, :, columns(1 - core, j)], qbuf.at[1, :, kept(j)],
                      q_send.at[j], q_recv.at[j], mate)

    def local_copies(j):
        mine = columns(core, j)
        return [
            pltpu.make_async_copy(q_hbm.at[0, :, mine], qbuf.at[0, :, kept(j)], q_local.at[j]),
            pltpu.make_async_copy(k_hbm.at[0, :, mine], kbuf.at[0, :, kept(j)], k_recv.at[0, j]),
            pltpu.make_async_copy(v_hbm.at[0, :, mine], vbuf.at[0, :, kept(j)], v_recv.at[0, j]),
        ]

    def o_copies(j):
        mine = columns(core, j)
        return [
            pltpu.make_async_copy(obuf.at[0, :, kept(j)], hid_hbm.at[:, mine], o_local.at[j]),
            remote(obuf.at[1, :, kept(j)], hid_hbm.at[:, mine], o_send.at[j], o_recv.at[j], mate),
        ]

    def piece(i):
        return pl.ds(i * piece_rows, piece_rows)

    def direct_copies(dx, dc):
        slot = ((chips - dx) % chips) * 2 + dc
        side = lax.rem(core + dc, 2)
        return [
            remote(src.at[0, piece(pieces - 1), columns(side, final)],
                   buf.at[slot, piece(pieces - 1), kept(final)],
                   send.at[slot, final], piece_recv.at[pieces - 1, slot, kind], peer(dx, dc))
            for kind, (src, buf, send) in enumerate(
                ((k_hbm, kbuf, k_send), (v_hbm, vbuf, v_send)))
        ]

    def out_copies(i):
        return [
            remote(src.at[0, piece(i), columns(side, final)], relay_in.at[kind, side],
                   in_send.at[i, kind, side], in_recv.at[kind, side],
                   me, comps - pieces + i)
            for kind, src in enumerate((k_hbm, v_hbm)) for side in range(2)
        ]

    def across_copies():
        copies = []
        for (dx, dc), slot in zip(far, far_slots):
            for kind in range(2):
                copies.append(remote(
                    relay_in.at[kind, lax.rem(core + dc, 2)], relay_mid.at[slot, kind],
                    mid_send.at[slot, kind], mid_recv.at[slot, kind], peer(dx, dc)))
        return copies

    def back_copies(i):
        return [
            remote(relay_mid.at[slot, kind], buf.at[slot, piece(i), kept(final)],
                   back_send.at[slot, kind], piece_recv.at[i, slot, kind], me, comps - 1)
            for slot in far_slots for kind, buf in enumerate((kbuf, vbuf))
        ]

    def piece_arrivals(i):
        return [
            pltpu.make_async_copy(buf.at[slot, piece(i), kept(final)],
                                  buf.at[slot, piece(i), kept(final)],
                                  piece_recv.at[i, slot, kind])
            for slot in far_slots for kind, buf in enumerate((kbuf, vbuf))
        ]

    w_side = me // chips
    w_slot = lax.rem(me, chips)

    def w_cols(i):
        return pl.ds(i * piece_cols, piece_cols)

    def w_near():
        return remote(w_hbm, wbuf.at[w_slot], w_send.at[chips], w_recv.at[w_slot],
                      chip * 2 + w_side)

    def w_direct(x):
        return remote(w_hbm.at[:, w_cols(w_pieces - 1)], wbuf.at[w_slot, :, w_cols(w_pieces - 1)],
                      w_send.at[x], w_piece.at[w_pieces - 1, w_slot], x * 2 + w_side)

    def w_across(i, x):
        return remote(w_hbm.at[:, w_cols(i)], w_mid.at[w_slot],
                      wm_send.at[x], wm_recv.at[w_slot], x * 2 + w_side)

    def w_back(i, x):
        return remote(w_mid.at[x], wbuf.at[x, :, w_cols(i)],
                      wb_send.at[x], w_piece.at[i, x], me, comps - 1)

    def is_near(slot):
        return (core * chips + slot) // 2 == chip

    @pl.when(last)
    def _():
        @pl.when(chip * 2 + w_side != me)
        def _():
            w_near().start()

        @pl.when(chip * 2 + w_side == me)
        def _():
            pltpu.make_async_copy(w_hbm, wbuf.at[w_slot], w_recv.at[w_slot]).start()

        for x in range(chips):
            @pl.when(x != chip)
            def _():
                w_direct(x).start()

        acc[...] = jnp.zeros_like(acc)
        sq[...] = jnp.zeros_like(sq)

    for i in range(w_pieces - 1):
        @pl.when(comp == comps - w_pieces + i)
        def _():
            for x in range(chips):
                @pl.when(x != chip)
                def _():
                    w_across(i, x).start()

    def start_chunk(j, carry):
        cut = jnp.logical_and(last, j == final)

        @pl.when(jnp.logical_not(cut))
        def _():
            for dx, dc in far:
                for copy in kv_copies(dx, dc, j):
                    copy.start()

        @pl.when(cut)
        def _():
            for dx, dc in far:
                for copy in direct_copies(dx, dc):
                    copy.start()

        for copy in kv_copies(0, 1, j):
            copy.start()
        q_copy(j).start()
        for copy in local_copies(j):
            copy.start()
        return carry

    lax.fori_loop(0, WINDOW, start_chunk, 0)

    @pl.when(last)
    def _():
        pl.semaphore_wait(ready, 2 * (comps - 1))
        for i in range(pieces - 1):
            for copy in out_copies(i):
                copy.start()

    def relay_across():
        @pl.when(helper)
        def _():
            for copy in out_copies(0):
                copy.wait_recv()
            for copy in across_copies():
                copy.start()

    def relay_back():
        @pl.when(helper)
        def _():
            for copy in across_copies():
                copy.wait_recv()
        for i in range(pieces - 1):
            @pl.when(comp == comps - pieces + i)
            def _():
                for copy in back_copies(i):
                    copy.start()
        for i in range(w_pieces - 1):
            @pl.when(comp == comps - w_pieces + i)
            def _():
                for x in range(chips):
                    @pl.when(jnp.logical_not(is_near(x)))
                    def _():
                        pltpu.make_async_copy(w_mid.at[x], w_mid.at[x], wm_recv.at[x]).wait()
                        w_back(i, x).start()

    def await_rows():
        for x in range(chips):
            @pl.when(is_near(x))
            def _():
                pltpu.make_async_copy(wbuf.at[x], wbuf.at[x], w_recv.at[x]).wait()

            @pl.when(jnp.logical_not(is_near(x)))
            def _():
                for i in range(w_pieces):
                    dst = wbuf.at[x, :, w_cols(i)]
                    pltpu.make_async_copy(dst, dst, w_piece.at[i, x]).wait()

    def project(j, carry):
        part = obuf[:, :, kept(j)].reshape(2 * tokens, cw)
        first = j * cw
        rows = wbuf[first // rows_w, :, pl.ds(pl.multiple_of(first % rows_w, cw), cw)]
        acc[...] += lax.dot_general(
            part, rows, (((1,), (1,)), ((), ())), preferred_element_type=jnp.float32
        )
        wide = part.astype(jnp.float32)
        sq[...] += jnp.sum(wide * wide, axis=1, keepdims=True)
        return carry

    factor = HD ** (-0.5) * math.log2(math.e)

    def attend(j, carry):
        for copy in local_copies(j):
            copy.wait()
        q_copy(j).wait_recv()
        for copy in kv_copies(0, 1, j):
            copy.wait_recv()
        cut = jnp.logical_and(last, j == final)

        @pl.when(jnp.logical_not(cut))
        def _():
            for dx, dc in far:
                for copy in kv_copies(dx, dc, j):
                    copy.wait_recv()

        @pl.when(cut)
        def _():
            for i in range(pieces):
                for copy in piece_arrivals(i):
                    copy.wait()

        pl.when(j == 1)(relay_across)
        pl.when(j == 3)(relay_back)

        @pl.when(j + WINDOW < CHUNKS)
        def _():
            start_chunk(j + WINDOW, 0)

        for h in range(cw // HD):
            cols = pl.ds(pl.multiple_of(j * cw + h * HD, HD), HD)
            query = qbuf[:, :, cols].reshape(2 * tokens, HD)
            key = kbuf[:, :, cols].reshape(n * tokens, HD)
            value = vbuf[:, :, cols].reshape(n * tokens, HD)
            scores = lax.dot_general(
                query, key, (((1,), (1,)), ((), ())), preferred_element_type=jnp.float32
            )
            highest = jnp.max(scores, axis=1, keepdims=True)
            weights = jnp.exp2((scores - highest) * factor)
            totals = jnp.sum(weights, axis=1, keepdims=True)
            out = jnp.dot(weights.astype(jnp.bfloat16), value, preferred_element_type=jnp.float32)
            out = (out / totals).astype(jnp.bfloat16)
            obuf[:, :, cols] = out.reshape(2, tokens, HD)
        for copy in o_copies(j):
            copy.start()

        @pl.when(jnp.logical_and(last, j == LATE))
        def _():
            await_rows()
            lax.fori_loop(0, LATE + 1, project, 0)

        @pl.when(jnp.logical_and(last, j > LATE))
        def _():
            project(j, 0)

        return carry

    lax.fori_loop(0, CHUNKS, attend, 0)

    def noise_copy(c, side):
        return pltpu.make_async_remote_copy(
            src_ref=nsend.at[c, side], dst_ref=nrecv.at[side],
            send_sem=n_send.at[c, side], recv_sem=n_recv.at[side],
            device_id=(c, me if side == 0 else mate), device_id_type=MESH,
        )

    def noise_self():
        return pltpu.make_async_copy(nsend.at[comps - 1, 0], nrecv.at[0], n_recv.at[0])

    @pl.when(last)
    def _():
        both = jnp.concatenate([acc[...], jnp.broadcast_to(sq[...], acc.shape)], axis=1).T
        channels = acc.shape[1]
        for c in range(comps):
            for side in range(2):
                toks = slice(side * tokens, (side + 1) * tokens)
                nsend[c, side, 0:own, :] = both[c * own:(c + 1) * own, toks]
                nsend[c, side, pad:pad + 8, :] = both[channels:channels + 8, toks]
        for c in range(comps):
            for side in range(2):
                if (c, side) == (comps - 1, 0):
                    noise_self().start()
                else:
                    noise_copy(c, side).start()

    def drain(j, carry):
        cut = jnp.logical_and(last, j == final)

        @pl.when(jnp.logical_not(cut))
        def _():
            for dx, dc in far:
                for copy in kv_copies(dx, dc, j):
                    copy.wait_send()

        @pl.when(cut)
        def _():
            for dx, dc in far:
                for copy in direct_copies(dx, dc):
                    copy.wait_send()

        for copy in kv_copies(0, 1, j):
            copy.wait_send()
        q_copy(j).wait_send()
        local, back = o_copies(j)
        local.wait()
        back.wait()
        return carry

    lax.fori_loop(0, CHUNKS, drain, 0)

    @pl.when(helper)
    def _():
        for copy in across_copies() + back_copies(0):
            copy.wait_send()

    @pl.when(w_helper)
    def _():
        for x in range(chips):
            @pl.when(x != chip)
            def _():
                w_across(0, x).wait_send()

            @pl.when(jnp.logical_not(is_near(x)))
            def _():
                w_back(0, x).wait_send()

    @pl.when(last)
    def _():
        @pl.when(chip * 2 + w_side != me)
        def _():
            w_near().wait_send()

        for x in range(chips):
            @pl.when(x != chip)
            def _():
                w_direct(x).wait_send()
        for i in range(pieces - 1):
            for copy in out_copies(i):
                copy.wait_send()
        for c in range(comps):
            for side in range(2):
                if (c, side) != (comps - 1, 0):
                    noise_copy(c, side).wait_send()

    for side in range(2):
        pltpu.make_async_copy(nsend.at[0, side], nrecv.at[side], n_recv.at[side]).wait()
    total = nrecv[0] + nrecv[1]
    root = jnp.sqrt(total[pad:pad + 1] / width + 1e-06)
    noise_ref[...] = total[0:own] / root


def on_device(queries, keys, values, latent, prev_denoised, head_weight):
    n = lax.axis_size("seq")
    comps = lax.axis_size("comp")
    _, tokens, width = queries.shape
    half = width // 2
    own = latent.shape[0]
    channels = head_weight.shape[1]
    pad = -(-own // 8) * 8
    chips, rows_w = n // 2, width // n
    pieces = min(comps, tokens // 16)
    w_pieces = min(comps, rows_w // 128)
    bf16, f32 = jnp.bfloat16, jnp.float32
    dma = pltpu.SemaphoreType.DMA
    anywhere = pl.BlockSpec(memory_space=pl.ANY)
    hidden, noise_own = pl.pallas_call(
        functools.partial(kernel, n, comps, own),
        out_shape=(
            pltpu.VMEM((tokens, width), bf16),
            pltpu.VMEM((own, tokens), f32),
        ),
        in_specs=[anywhere] * 4,
        out_specs=(anywhere, pl.BlockSpec(memory_space=pltpu.VMEM)),
        scratch_shapes=[
            pltpu.VMEM((n, tokens, half), bf16),
            pltpu.VMEM((n, tokens, half), bf16),
            pltpu.VMEM((2, tokens, half), bf16),
            pltpu.VMEM((2, tokens, half), bf16),
            pltpu.VMEM((n // 2, channels, width // n), bf16),
            pltpu.VMEM((2 * tokens, channels), f32),
            pltpu.VMEM((2 * tokens, 1), f32),
            pltpu.VMEM((comps, 2, pad + 8, tokens), f32),
            pltpu.VMEM((2, pad + 8, tokens), f32),
            pltpu.VMEM((2, 2, tokens // pieces, half // CHUNKS), bf16),
            pltpu.VMEM((n, 2, tokens // pieces, half // CHUNKS), bf16),
            pltpu.VMEM((chips, channels, rows_w // w_pieces), bf16),
            dma((n, CHUNKS)), dma((n, CHUNKS)), dma((n, CHUNKS)), dma((n, CHUNKS)),
            dma((CHUNKS,)), dma((CHUNKS,)), dma((CHUNKS,)),
            dma((CHUNKS,)), dma((CHUNKS,)), dma((CHUNKS,)),
            dma((chips + 1,)), dma((chips,)),
            dma((comps, 2)), dma((2,)),
            dma((pieces, 2, 2)), dma((2, 2)), dma((n, 2)), dma((n, 2)), dma((n, 2)),
            dma((pieces, n, 2)),
            dma((chips,)), dma((chips,)), dma((chips,)), dma((w_pieces, chips)),
            pltpu.SemaphoreType.REGULAR,
        ],
        compiler_params=pltpu.CompilerParams(
            collective_id=0, has_side_effects=True, vmem_limit_bytes=60 * 1024 * 1024
        ),
        name="attention_step",
    )(queries, keys, values, head_weight.T)
    denoised = (latent - sigma_now * noise_own) / alpha_now
    step_now = math.log(alpha_next / sigma_next) - math.log(alpha_now / sigma_now)
    ratio = step_before / step_now
    blend = (1.0 + 0.5 / ratio) * denoised - 0.5 / ratio * prev_denoised
    new_latent = sigma_next / sigma_now * latent - alpha_next * (math.exp(-step_now) - 1.0) * blend
    return (hidden[None], new_latent, denoised)


def solution(mesh):
    return jax.shard_map(
        on_device,
        mesh=mesh,
        in_specs=(
            P("comp", "seq", None),
            P("comp", "seq", None),
            P("comp", "seq", None),
            P("comp", "seq"),
            P("comp", "seq"),
            P("seq", None),
        ),
        out_specs=(P("comp", "seq", None), P("comp", "seq"), P("comp", "seq")),
        check_vma=False,
    )
```

```python
import functools
import math

import jax
import jax.numpy as jnp
from jax import lax
from jax.experimental import pallas as pl
from jax.experimental.pallas import tpu as pltpu
from jax.sharding import PartitionSpec as P

HD = 128
CHUNKS = 8
WINDOW = 2
LATE = 5
MESH = pl.DeviceIdType.MESH

alpha_now = 0.6
sigma_now = 0.8
alpha_next = 0.8
sigma_next = 0.6
step_before = 0.4


def kernel(
    n, comps, own, q_hbm, k_hbm, v_hbm, w_hbm, hid_hbm, noise_ref,
    kbuf, vbuf, qbuf, obuf, wbuf, acc, sq, nsend, nrecv, relay_in, relay_mid, w_mid,
    k_send, k_recv, v_send, v_recv, q_send, q_recv, q_local,
    o_send, o_recv, o_local, w_send, w_recv, n_send, n_recv,
    in_send, in_recv, mid_send, mid_recv, back_send, piece_recv,
    wm_send, wm_recv, wb_send, w_piece,
):
    tokens, width = hid_hbm.shape
    half = width // 2
    chips = n // 2
    cw = half // CHUNKS
    rows_w = width // n
    pad = nsend.shape[2] - 8
    comp = lax.axis_index("comp")
    me = lax.axis_index("seq")
    chip, core = me // 2, me % 2
    mate = chip * 2 + 1 - core
    last = comp == comps - 1

    def peer(d_chip, d_core):
        return lax.rem(chip + d_chip, chips) * 2 + lax.rem(core + d_core, 2)

    barrier = pltpu.get_barrier_semaphore()
    others = [(dx, dc) for dx in range(chips) for dc in range(2) if (dx, dc) != (0, 0)]
    for dx, dc in others:
        pl.semaphore_signal(barrier, inc=1, device_id=(comp, peer(dx, dc)), device_id_type=MESH)

    @pl.when(jnp.logical_not(last))
    def _():
        for target in (me, mate):
            pl.semaphore_signal(
                barrier, inc=1, device_id=(comps - 1, target), device_id_type=MESH
            )
        pl.semaphore_wait(barrier, n - 1)

    @pl.when(last)
    def _():
        pl.semaphore_wait(barrier, n - 1 + 2 * (comps - 1))

    pieces, piece_rows = piece_recv.shape[0], relay_in.shape[2]
    w_pieces, piece_cols = w_piece.shape[0], w_mid.shape[2]
    helper = jnp.logical_and(jnp.logical_not(last), comp >= comps - pieces)
    w_helper = jnp.logical_and(jnp.logical_not(last), comp >= comps - w_pieces)
    final = CHUNKS - 1
    far = [(dx, dc) for dx in range(1, chips) for dc in range(2)]
    far_slots = [((chips - dx) % chips) * 2 + dc for dx, dc in far]

    def columns(side, j):
        return pl.ds(pl.multiple_of(side * half + j * cw, cw), cw)

    def kept(j):
        return pl.ds(pl.multiple_of(j * cw, cw), cw)

    def remote(src, dst, send, recv, target, owner=comp):
        return pltpu.make_async_remote_copy(
            src_ref=src, dst_ref=dst, send_sem=send, recv_sem=recv,
            device_id=(owner, target), device_id_type=MESH,
        )

    def kv_copies(dx, dc, j):
        target = peer(dx, dc)
        side = lax.rem(core + dc, 2)
        slot = ((chips - dx) % chips) * 2 + dc
        return [
            remote(src.at[0, :, columns(side, j)], buf.at[slot, :, kept(j)],
                   send.at[slot, j], recv.at[slot, j], target)
            for src, buf, send, recv in (
                (k_hbm, kbuf, k_send, k_recv), (v_hbm, vbuf, v_send, v_recv))
        ]

    def q_copy(j):
        return remote(q_hbm.at[0, :, columns(1 - core, j)], qbuf.at[1, :, kept(j)],
                      q_send.at[j], q_recv.at[j], mate)

    def local_copies(j):
        mine = columns(core, j)
        return [
            pltpu.make_async_copy(q_hbm.at[0, :, mine], qbuf.at[0, :, kept(j)], q_local.at[j]),
            pltpu.make_async_copy(k_hbm.at[0, :, mine], kbuf.at[0, :, kept(j)], k_recv.at[0, j]),
            pltpu.make_async_copy(v_hbm.at[0, :, mine], vbuf.at[0, :, kept(j)], v_recv.at[0, j]),
        ]

    def o_copies(j):
        mine = columns(core, j)
        return [
            pltpu.make_async_copy(obuf.at[0, :, kept(j)], hid_hbm.at[:, mine], o_local.at[j]),
            remote(obuf.at[1, :, kept(j)], hid_hbm.at[:, mine], o_send.at[j], o_recv.at[j], mate),
        ]

    def piece(i):
        return pl.ds(i * piece_rows, piece_rows)

    def direct_copies(dx, dc):
        slot = ((chips - dx) % chips) * 2 + dc
        side = lax.rem(core + dc, 2)
        return [
            remote(src.at[0, piece(pieces - 1), columns(side, final)],
                   buf.at[slot, piece(pieces - 1), kept(final)],
                   send.at[slot, final], piece_recv.at[pieces - 1, slot, kind], peer(dx, dc))
            for kind, (src, buf, send) in enumerate(
                ((k_hbm, kbuf, k_send), (v_hbm, vbuf, v_send)))
        ]

    def out_copies(i):
        return [
            remote(src.at[0, piece(i), columns(side, final)], relay_in.at[kind, side],
                   in_send.at[i, kind, side], in_recv.at[kind, side],
                   me, comps - pieces + i)
            for kind, src in enumerate((k_hbm, v_hbm)) for side in range(2)
        ]

    def across_copies():
        copies = []
        for (dx, dc), slot in zip(far, far_slots):
            for kind in range(2):
                copies.append(remote(
                    relay_in.at[kind, lax.rem(core + dc, 2)], relay_mid.at[slot, kind],
                    mid_send.at[slot, kind], mid_recv.at[slot, kind], peer(dx, dc)))
        return copies

    def back_copies(i):
        return [
            remote(relay_mid.at[slot, kind], buf.at[slot, piece(i), kept(final)],
                   back_send.at[slot, kind], piece_recv.at[i, slot, kind], me, comps - 1)
            for slot in far_slots for kind, buf in enumerate((kbuf, vbuf))
        ]

    def piece_arrivals(i):
        return [
            pltpu.make_async_copy(buf.at[slot, piece(i), kept(final)],
                                  buf.at[slot, piece(i), kept(final)],
                                  piece_recv.at[i, slot, kind])
            for slot in far_slots for kind, buf in enumerate((kbuf, vbuf))
        ]

    w_side = me // chips
    w_slot = lax.rem(me, chips)

    def w_cols(i):
        return pl.ds(i * piece_cols, piece_cols)

    def w_near():
        return remote(w_hbm, wbuf.at[w_slot], w_send.at[chips], w_recv.at[w_slot],
                      chip * 2 + w_side)

    def w_direct(x):
        return remote(w_hbm.at[:, w_cols(w_pieces - 1)], wbuf.at[w_slot, :, w_cols(w_pieces - 1)],
                      w_send.at[x], w_piece.at[w_pieces - 1, w_slot], x * 2 + w_side)

    def w_across(i, x):
        return remote(w_hbm.at[:, w_cols(i)], w_mid.at[w_slot],
                      wm_send.at[x], wm_recv.at[w_slot], x * 2 + w_side)

    def w_back(i, x):
        return remote(w_mid.at[x], wbuf.at[x, :, w_cols(i)],
                      wb_send.at[x], w_piece.at[i, x], me, comps - 1)

    def is_near(slot):
        return (core * chips + slot) // 2 == chip

    @pl.when(last)
    def _():
        @pl.when(chip * 2 + w_side != me)
        def _():
            w_near().start()

        @pl.when(chip * 2 + w_side == me)
        def _():
            pltpu.make_async_copy(w_hbm, wbuf.at[w_slot], w_recv.at[w_slot]).start()

        for x in range(chips):
            @pl.when(x != chip)
            def _():
                w_direct(x).start()

        acc[...] = jnp.zeros_like(acc)
        sq[...] = jnp.zeros_like(sq)

    for i in range(w_pieces - 1):
        @pl.when(comp == comps - w_pieces + i)
        def _():
            for x in range(chips):
                @pl.when(x != chip)
                def _():
                    w_across(i, x).start()

    def start_chunk(j, carry):
        cut = jnp.logical_and(last, j == final)

        @pl.when(jnp.logical_not(cut))
        def _():
            for dx, dc in far:
                for copy in kv_copies(dx, dc, j):
                    copy.start()

        @pl.when(cut)
        def _():
            for dx, dc in far:
                for copy in direct_copies(dx, dc):
                    copy.start()

        for copy in kv_copies(0, 1, j):
            copy.start()
        q_copy(j).start()
        for copy in local_copies(j):
            copy.start()
        return carry

    lax.fori_loop(0, WINDOW, start_chunk, 0)

    @pl.when(last)
    def _():
        for i in range(pieces - 1):
            for copy in out_copies(i):
                copy.start()

    def relay_across():
        @pl.when(helper)
        def _():
            for copy in out_copies(0):
                copy.wait_recv()
            for copy in across_copies():
                copy.start()

    def relay_back():
        @pl.when(helper)
        def _():
            for copy in across_copies():
                copy.wait_recv()
        for i in range(pieces - 1):
            @pl.when(comp == comps - pieces + i)
            def _():
                for copy in back_copies(i):
                    copy.start()
        for i in range(w_pieces - 1):
            @pl.when(comp == comps - w_pieces + i)
            def _():
                for x in range(chips):
                    @pl.when(jnp.logical_not(is_near(x)))
                    def _():
                        pltpu.make_async_copy(w_mid.at[x], w_mid.at[x], wm_recv.at[x]).wait()
                        w_back(i, x).start()

    def await_rows():
        for x in range(chips):
            @pl.when(is_near(x))
            def _():
                pltpu.make_async_copy(wbuf.at[x], wbuf.at[x], w_recv.at[x]).wait()

            @pl.when(jnp.logical_not(is_near(x)))
            def _():
                for i in range(w_pieces):
                    dst = wbuf.at[x, :, w_cols(i)]
                    pltpu.make_async_copy(dst, dst, w_piece.at[i, x]).wait()

    def project(j, carry):
        part = obuf[:, :, kept(j)].reshape(2 * tokens, cw)
        first = j * cw
        rows = wbuf[first // rows_w, :, pl.ds(pl.multiple_of(first % rows_w, cw), cw)]
        acc[...] += lax.dot_general(
            part, rows, (((1,), (1,)), ((), ())), preferred_element_type=jnp.float32
        )
        wide = part.astype(jnp.float32)
        sq[...] += jnp.sum(wide * wide, axis=1, keepdims=True)
        return carry

    factor = HD ** (-0.5) * math.log2(math.e)

    def attend(j, carry):
        for copy in local_copies(j):
            copy.wait()
        q_copy(j).wait_recv()
        for copy in kv_copies(0, 1, j):
            copy.wait_recv()
        cut = jnp.logical_and(last, j == final)

        @pl.when(jnp.logical_not(cut))
        def _():
            for dx, dc in far:
                for copy in kv_copies(dx, dc, j):
                    copy.wait_recv()

        @pl.when(cut)
        def _():
            for i in range(pieces):
                for copy in piece_arrivals(i):
                    copy.wait()

        pl.when(j == 1)(relay_across)
        pl.when(j == 3)(relay_back)

        @pl.when(j + WINDOW < CHUNKS)
        def _():
            start_chunk(j + WINDOW, 0)

        for h in range(cw // HD):
            cols = pl.ds(pl.multiple_of(j * cw + h * HD, HD), HD)
            query = qbuf[:, :, cols].reshape(2 * tokens, HD)
            key = kbuf[:, :, cols].reshape(n * tokens, HD)
            value = vbuf[:, :, cols].reshape(n * tokens, HD)
            scores = lax.dot_general(
                query, key, (((1,), (1,)), ((), ())), preferred_element_type=jnp.float32
            )
            highest = jnp.max(scores, axis=1, keepdims=True)
            weights = jnp.exp2((scores - highest) * factor)
            totals = jnp.sum(weights, axis=1, keepdims=True)
            out = jnp.dot(weights.astype(jnp.bfloat16), value, preferred_element_type=jnp.float32)
            out = (out / totals).astype(jnp.bfloat16)
            obuf[:, :, cols] = out.reshape(2, tokens, HD)
        for copy in o_copies(j):
            copy.start()

        @pl.when(jnp.logical_and(last, j == LATE))
        def _():
            await_rows()
            lax.fori_loop(0, LATE + 1, project, 0)

        @pl.when(jnp.logical_and(last, j > LATE))
        def _():
            project(j, 0)

        return carry

    lax.fori_loop(0, CHUNKS, attend, 0)

    def noise_copy(c, side):
        return pltpu.make_async_remote_copy(
            src_ref=nsend.at[c, side], dst_ref=nrecv.at[side],
            send_sem=n_send.at[c, side], recv_sem=n_recv.at[side],
            device_id=(c, me if side == 0 else mate), device_id_type=MESH,
        )

    def noise_self():
        return pltpu.make_async_copy(nsend.at[comps - 1, 0], nrecv.at[0], n_recv.at[0])

    @pl.when(last)
    def _():
        both = jnp.concatenate([acc[...], jnp.broadcast_to(sq[...], acc.shape)], axis=1).T
        channels = acc.shape[1]
        for c in range(comps):
            for side in range(2):
                toks = slice(side * tokens, (side + 1) * tokens)
                nsend[c, side, 0:own, :] = both[c * own:(c + 1) * own, toks]
                nsend[c, side, pad:pad + 8, :] = both[channels:channels + 8, toks]
        for c in range(comps):
            for side in range(2):
                if (c, side) == (comps - 1, 0):
                    noise_self().start()
                else:
                    noise_copy(c, side).start()

    def drain(j, carry):
        cut = jnp.logical_and(last, j == final)

        @pl.when(jnp.logical_not(cut))
        def _():
            for dx, dc in far:
                for copy in kv_copies(dx, dc, j):
                    copy.wait_send()

        @pl.when(cut)
        def _():
            for dx, dc in far:
                for copy in direct_copies(dx, dc):
                    copy.wait_send()

        for copy in kv_copies(0, 1, j):
            copy.wait_send()
        q_copy(j).wait_send()
        local, back = o_copies(j)
        local.wait()
        back.wait()
        return carry

    lax.fori_loop(0, CHUNKS, drain, 0)

    @pl.when(helper)
    def _():
        for copy in across_copies() + back_copies(0):
            copy.wait_send()

    @pl.when(w_helper)
    def _():
        for x in range(chips):
            @pl.when(x != chip)
            def _():
                w_across(0, x).wait_send()

            @pl.when(jnp.logical_not(is_near(x)))
            def _():
                w_back(0, x).wait_send()

    @pl.when(last)
    def _():
        @pl.when(chip * 2 + w_side != me)
        def _():
            w_near().wait_send()

        for x in range(chips):
            @pl.when(x != chip)
            def _():
                w_direct(x).wait_send()
        for i in range(pieces - 1):
            for copy in out_copies(i):
                copy.wait_send()
        for c in range(comps):
            for side in range(2):
                if (c, side) != (comps - 1, 0):
                    noise_copy(c, side).wait_send()

    for side in range(2):
        pltpu.make_async_copy(nsend.at[0, side], nrecv.at[side], n_recv.at[side]).wait()
    total = nrecv[0] + nrecv[1]
    root = jnp.sqrt(total[pad:pad + 1] / width + 1e-06)
    noise_ref[...] = total[0:own] / root


def on_device(queries, keys, values, latent, prev_denoised, head_weight):
    n = lax.axis_size("seq")
    comps = lax.axis_size("comp")
    _, tokens, width = queries.shape
    half = width // 2
    own = latent.shape[0]
    channels = head_weight.shape[1]
    pad = -(-own // 8) * 8
    chips, rows_w = n // 2, width // n
    pieces = min(comps, tokens // 16)
    w_pieces = min(comps, rows_w // 128)
    bf16, f32 = jnp.bfloat16, jnp.float32
    dma = pltpu.SemaphoreType.DMA
    anywhere = pl.BlockSpec(memory_space=pl.ANY)
    hidden, noise_own = pl.pallas_call(
        functools.partial(kernel, n, comps, own),
        out_shape=(
            pltpu.VMEM((tokens, width), bf16),
            pltpu.VMEM((own, tokens), f32),
        ),
        in_specs=[anywhere] * 4,
        out_specs=(anywhere, pl.BlockSpec(memory_space=pltpu.VMEM)),
        scratch_shapes=[
            pltpu.VMEM((n, tokens, half), bf16),
            pltpu.VMEM((n, tokens, half), bf16),
            pltpu.VMEM((2, tokens, half), bf16),
            pltpu.VMEM((2, tokens, half), bf16),
            pltpu.VMEM((n // 2, channels, width // n), bf16),
            pltpu.VMEM((2 * tokens, channels), f32),
            pltpu.VMEM((2 * tokens, 1), f32),
            pltpu.VMEM((comps, 2, pad + 8, tokens), f32),
            pltpu.VMEM((2, pad + 8, tokens), f32),
            pltpu.VMEM((2, 2, tokens // pieces, half // CHUNKS), bf16),
            pltpu.VMEM((n, 2, tokens // pieces, half // CHUNKS), bf16),
            pltpu.VMEM((chips, channels, rows_w // w_pieces), bf16),
            dma((n, CHUNKS)), dma((n, CHUNKS)), dma((n, CHUNKS)), dma((n, CHUNKS)),
            dma((CHUNKS,)), dma((CHUNKS,)), dma((CHUNKS,)),
            dma((CHUNKS,)), dma((CHUNKS,)), dma((CHUNKS,)),
            dma((chips + 1,)), dma((chips,)),
            dma((comps, 2)), dma((2,)),
            dma((pieces, 2, 2)), dma((2, 2)), dma((n, 2)), dma((n, 2)), dma((n, 2)),
            dma((pieces, n, 2)),
            dma((chips,)), dma((chips,)), dma((chips,)), dma((w_pieces, chips)),
        ],
        compiler_params=pltpu.CompilerParams(
            collective_id=0, has_side_effects=True, vmem_limit_bytes=60 * 1024 * 1024
        ),
        name="attention_step",
    )(queries, keys, values, head_weight.T)
    denoised = (latent - sigma_now * noise_own) / alpha_now
    step_now = math.log(alpha_next / sigma_next) - math.log(alpha_now / sigma_now)
    ratio = step_before / step_now
    blend = (1.0 + 0.5 / ratio) * denoised - 0.5 / ratio * prev_denoised
    new_latent = sigma_next / sigma_now * latent - alpha_next * (math.exp(-step_now) - 1.0) * blend
    return (hidden[None], new_latent, denoised)


def solution(mesh):
    return jax.shard_map(
        on_device,
        mesh=mesh,
        in_specs=(
            P("comp", "seq", None),
            P("comp", "seq", None),
            P("comp", "seq", None),
            P("comp", "seq"),
            P("comp", "seq"),
            P("seq", None),
        ),
        out_specs=(P("comp", "seq", None), P("comp", "seq"), P("comp", "seq")),
        check_vma=False,
    )
```

```python
import functools
import math

import jax
import jax.numpy as jnp
from jax import lax
from jax.experimental import pallas as pl
from jax.experimental.pallas import tpu as pltpu
from jax.sharding import PartitionSpec as P

HD = 128
SIZES = (4, 4, 4, 2, 1, 1)
CHUNKS = len(SIZES)
FIRST = tuple(sum(SIZES[:j]) for j in range(CHUNKS))
FINAL = 3
LATE = 3
STARTS = {0: (2,), 1: (3,), 2: (4, 5)}
MESH = pl.DeviceIdType.MESH

alpha_now = 0.6
sigma_now = 0.8
alpha_next = 0.8
sigma_next = 0.6
step_before = 0.4


def kernel(
    n, comps, own, q_hbm, k_hbm, v_hbm, w_hbm, hid_hbm, noise_ref,
    kbuf, vbuf, qbuf, obuf, wbuf, acc, sq, nsend, nrecv, relay_in, relay_mid, w_mid,
    k_send, k_recv, v_send, v_recv, q_send, q_recv, q_local,
    o_send, o_recv, o_local, w_send, w_recv, n_send, n_recv,
    in_send, in_recv, mid_send, mid_recv, back_send, piece_recv,
    wm_send, wm_recv, wb_send, w_piece,
):
    tokens, width = hid_hbm.shape
    half = width // 2
    chips = n // 2
    assert sum(SIZES) * HD == half
    rows_w = width // n
    pad = nsend.shape[2] - 8
    comp = lax.axis_index("comp")
    me = lax.axis_index("seq")
    chip, core = me // 2, me % 2
    mate = chip * 2 + 1 - core
    last = comp == comps - 1

    def peer(d_chip, d_core):
        return lax.rem(chip + d_chip, chips) * 2 + lax.rem(core + d_core, 2)

    barrier = pltpu.get_barrier_semaphore()
    others = [(dx, dc) for dx in range(chips) for dc in range(2) if (dx, dc) != (0, 0)]
    for dx, dc in others:
        pl.semaphore_signal(barrier, inc=1, device_id=(comp, peer(dx, dc)), device_id_type=MESH)

    @pl.when(jnp.logical_not(last))
    def _():
        for target in (me, mate):
            pl.semaphore_signal(
                barrier, inc=1, device_id=(comps - 1, target), device_id_type=MESH
            )
        pl.semaphore_wait(barrier, n - 1)

    @pl.when(last)
    def _():
        pl.semaphore_wait(barrier, n - 1 + 2 * (comps - 1))

    pieces, piece_rows = piece_recv.shape[0], relay_in.shape[2]
    w_pieces, piece_cols = w_piece.shape[0], w_mid.shape[2]
    helper = jnp.logical_and(jnp.logical_not(last), comp >= comps - pieces)
    w_helper = jnp.logical_and(jnp.logical_not(last), comp >= comps - w_pieces)
    final = FINAL
    far = [(dx, dc) for dx in range(1, chips) for dc in range(2)]
    far_slots = [((chips - dx) % chips) * 2 + dc for dx, dc in far]

    def columns(side, j):
        start = pl.multiple_of(side * half + FIRST[j] * HD, HD)
        return pl.ds(start, SIZES[j] * HD)

    def kept(j):
        return pl.ds(FIRST[j] * HD, SIZES[j] * HD)

    def remote(src, dst, send, recv, target, owner=comp):
        return pltpu.make_async_remote_copy(
            src_ref=src, dst_ref=dst, send_sem=send, recv_sem=recv,
            device_id=(owner, target), device_id_type=MESH,
        )

    def kv_copies(dx, dc, j):
        target = peer(dx, dc)
        side = lax.rem(core + dc, 2)
        slot = ((chips - dx) % chips) * 2 + dc
        return [
            remote(src.at[0, :, columns(side, j)], buf.at[slot, :, kept(j)],
                   send.at[slot, j], recv.at[slot, j], target)
            for src, buf, send, recv in (
                (k_hbm, kbuf, k_send, k_recv), (v_hbm, vbuf, v_send, v_recv))
        ]

    def q_copy(j):
        return remote(q_hbm.at[0, :, columns(1 - core, j)], qbuf.at[1, :, kept(j)],
                      q_send.at[j], q_recv.at[j], mate)

    def local_copies(j):
        mine = columns(core, j)
        return [
            pltpu.make_async_copy(q_hbm.at[0, :, mine], qbuf.at[0, :, kept(j)], q_local.at[j]),
            pltpu.make_async_copy(k_hbm.at[0, :, mine], kbuf.at[0, :, kept(j)], k_recv.at[0, j]),
            pltpu.make_async_copy(v_hbm.at[0, :, mine], vbuf.at[0, :, kept(j)], v_recv.at[0, j]),
        ]

    def o_copies(j):
        mine = columns(core, j)
        return [
            pltpu.make_async_copy(obuf.at[0, :, kept(j)], hid_hbm.at[:, mine], o_local.at[j]),
            remote(obuf.at[1, :, kept(j)], hid_hbm.at[:, mine], o_send.at[j], o_recv.at[j], mate),
        ]

    def piece(i):
        return pl.ds(i * piece_rows, piece_rows)

    def direct_copies(dx, dc):
        slot = ((chips - dx) % chips) * 2 + dc
        side = lax.rem(core + dc, 2)
        return [
            remote(src.at[0, piece(pieces - 1), columns(side, final)],
                   buf.at[slot, piece(pieces - 1), kept(final)],
                   send.at[slot, final], piece_recv.at[pieces - 1, slot, kind], peer(dx, dc))
            for kind, (src, buf, send) in enumerate(
                ((k_hbm, kbuf, k_send), (v_hbm, vbuf, v_send)))
        ]

    def out_copies(i):
        return [
            remote(src.at[0, piece(i), columns(side, final)], relay_in.at[kind, side],
                   in_send.at[i, kind, side], in_recv.at[kind, side],
                   me, comps - pieces + i)
            for kind, src in enumerate((k_hbm, v_hbm)) for side in range(2)
        ]

    def across_copies():
        copies = []
        for (dx, dc), slot in zip(far, far_slots):
            for kind in range(2):
                copies.append(remote(
                    relay_in.at[kind, lax.rem(core + dc, 2)], relay_mid.at[slot, kind],
                    mid_send.at[slot, kind], mid_recv.at[slot, kind], peer(dx, dc)))
        return copies

    def back_copies(i):
        return [
            remote(relay_mid.at[slot, kind], buf.at[slot, piece(i), kept(final)],
                   back_send.at[slot, kind], piece_recv.at[i, slot, kind], me, comps - 1)
            for slot in far_slots for kind, buf in enumerate((kbuf, vbuf))
        ]

    def piece_arrivals(i):
        return [
            pltpu.make_async_copy(buf.at[slot, piece(i), kept(final)],
                                  buf.at[slot, piece(i), kept(final)],
                                  piece_recv.at[i, slot, kind])
            for slot in far_slots for kind, buf in enumerate((kbuf, vbuf))
        ]

    w_side = me // chips
    w_slot = lax.rem(me, chips)

    def w_cols(i):
        return pl.ds(i * piece_cols, piece_cols)

    def w_near():
        return remote(w_hbm, wbuf.at[w_slot], w_send.at[chips], w_recv.at[w_slot],
                      chip * 2 + w_side)

    def w_direct(x):
        return remote(w_hbm.at[:, w_cols(w_pieces - 1)], wbuf.at[w_slot, :, w_cols(w_pieces - 1)],
                      w_send.at[x], w_piece.at[w_pieces - 1, w_slot], x * 2 + w_side)

    def w_across(i, x):
        return remote(w_hbm.at[:, w_cols(i)], w_mid.at[w_slot],
                      wm_send.at[x], wm_recv.at[w_slot], x * 2 + w_side)

    def w_back(i, x):
        return remote(w_mid.at[x], wbuf.at[x, :, w_cols(i)],
                      wb_send.at[x], w_piece.at[i, x], me, comps - 1)

    def is_near(slot):
        return (core * chips + slot) // 2 == chip

    @pl.when(last)
    def _():
        @pl.when(chip * 2 + w_side != me)
        def _():
            w_near().start()

        @pl.when(chip * 2 + w_side == me)
        def _():
            pltpu.make_async_copy(w_hbm, wbuf.at[w_slot], w_recv.at[w_slot]).start()

        for x in range(chips):
            @pl.when(x != chip)
            def _():
                w_direct(x).start()

        acc[...] = jnp.zeros_like(acc)
        sq[...] = jnp.zeros_like(sq)

    for i in range(w_pieces - 1):
        @pl.when(comp == comps - w_pieces + i)
        def _():
            for x in range(chips):
                @pl.when(x != chip)
                def _():
                    w_across(i, x).start()

    def start_far(j):
        for dx, dc in far:
            for copy in kv_copies(dx, dc, j):
                copy.start()

    def start_chunk(j):
        if j == final:
            @pl.when(jnp.logical_not(last))
            def _():
                start_far(j)

            @pl.when(last)
            def _():
                for dx, dc in far:
                    for copy in direct_copies(dx, dc):
                        copy.start()
        else:
            start_far(j)
        for copy in kv_copies(0, 1, j):
            copy.start()
        q_copy(j).start()
        for copy in local_copies(j):
            copy.start()

    start_chunk(0)
    start_chunk(1)

    @pl.when(last)
    def _():
        for i in range(pieces - 1):
            for copy in out_copies(i):
                copy.start()

    def relay_across():
        @pl.when(helper)
        def _():
            for copy in out_copies(0):
                copy.wait_recv()
            for copy in across_copies():
                copy.start()

    def relay_back():
        @pl.when(helper)
        def _():
            for copy in across_copies():
                copy.wait_recv()
        for i in range(pieces - 1):
            @pl.when(comp == comps - pieces + i)
            def _():
                for copy in back_copies(i):
                    copy.start()
        for i in range(w_pieces - 1):
            @pl.when(comp == comps - w_pieces + i)
            def _():
                for x in range(chips):
                    @pl.when(jnp.logical_not(is_near(x)))
                    def _():
                        pltpu.make_async_copy(w_mid.at[x], w_mid.at[x], wm_recv.at[x]).wait()
                        w_back(i, x).start()

    def await_rows():
        for x in range(chips):
            @pl.when(is_near(x))
            def _():
                pltpu.make_async_copy(wbuf.at[x], wbuf.at[x], w_recv.at[x]).wait()

            @pl.when(jnp.logical_not(is_near(x)))
            def _():
                for i in range(w_pieces):
                    dst = wbuf.at[x, :, w_cols(i)]
                    pltpu.make_async_copy(dst, dst, w_piece.at[i, x]).wait()

    def project(j):
        unit = min(SIZES[j], 2) * HD
        for first in range(FIRST[j] * HD, (FIRST[j] + SIZES[j]) * HD, unit):
            part = obuf[:, :, first:first + unit].reshape(2 * tokens, unit)
            at = first % rows_w
            rows = wbuf[first // rows_w, :, at:at + unit]
            acc[...] += lax.dot_general(
                part, rows, (((1,), (1,)), ((), ())), preferred_element_type=jnp.float32
            )
            wide = part.astype(jnp.float32)
            sq[...] += jnp.sum(wide * wide, axis=1, keepdims=True)

    factor = HD ** (-0.5) * math.log2(math.e)

    def wait_far(j):
        for dx, dc in far:
            for copy in kv_copies(dx, dc, j):
                copy.wait_recv()

    def attend(j):
        for copy in local_copies(j):
            copy.wait()
        q_copy(j).wait_recv()
        for copy in kv_copies(0, 1, j):
            copy.wait_recv()
        if j == final:
            @pl.when(jnp.logical_not(last))
            def _():
                wait_far(j)

            @pl.when(last)
            def _():
                for i in range(pieces):
                    for copy in piece_arrivals(i):
                        copy.wait()
        else:
            wait_far(j)

        if j == 1:
            relay_across()
        if j == 2:
            relay_back()
        for later in STARTS.get(j, ()):
            start_chunk(later)

        step = min(SIZES[j], 2)

        def heads(turn, carry):
            for h in range(step):
                at = (FIRST[j] + turn * step + h) * HD
                cols = pl.ds(pl.multiple_of(at, HD), HD)
                query = qbuf[:, :, cols].reshape(2 * tokens, HD)
                key = kbuf[:, :, cols].reshape(n * tokens, HD)
                value = vbuf[:, :, cols].reshape(n * tokens, HD)
                scores = lax.dot_general(
                    query, key, (((1,), (1,)), ((), ())), preferred_element_type=jnp.float32
                )
                highest = jnp.max(scores, axis=1, keepdims=True)
                weights = jnp.exp2((scores - highest) * factor)
                totals = jnp.sum(weights, axis=1, keepdims=True)
                out = jnp.dot(
                    weights.astype(jnp.bfloat16), value, preferred_element_type=jnp.float32
                )
                out = (out / totals).astype(jnp.bfloat16)
                obuf[:, :, cols] = out.reshape(2, tokens, HD)
            return carry

        lax.fori_loop(0, SIZES[j] // step, heads, 0)
        for copy in o_copies(j):
            copy.start()

        if j >= LATE:
            @pl.when(last)
            def _():
                if j == LATE:
                    await_rows()
                for done in range(0 if j == LATE else j, j + 1):
                    project(done)

    for j in range(CHUNKS):
        attend(j)

    def noise_copy(c, side):
        return pltpu.make_async_remote_copy(
            src_ref=nsend.at[c, side], dst_ref=nrecv.at[side],
            send_sem=n_send.at[c, side], recv_sem=n_recv.at[side],
            device_id=(c, me if side == 0 else mate), device_id_type=MESH,
        )

    def noise_self():
        return pltpu.make_async_copy(nsend.at[comps - 1, 0], nrecv.at[0], n_recv.at[0])

    @pl.when(last)
    def _():
        both = jnp.concatenate([acc[...], jnp.broadcast_to(sq[...], acc.shape)], axis=1).T
        channels = acc.shape[1]
        for c in range(comps):
            for side in range(2):
                toks = slice(side * tokens, (side + 1) * tokens)
                nsend[c, side, 0:own, :] = both[c * own:(c + 1) * own, toks]
                nsend[c, side, pad:pad + 8, :] = both[channels:channels + 8, toks]
        for c in range(comps):
            for side in range(2):
                if (c, side) == (comps - 1, 0):
                    noise_self().start()
                else:
                    noise_copy(c, side).start()

    def drain_far(j):
        for dx, dc in far:
            for copy in kv_copies(dx, dc, j):
                copy.wait_send()

    for j in range(CHUNKS):
        if j == final:
            @pl.when(jnp.logical_not(last))
            def _():
                drain_far(final)

            @pl.when(last)
            def _():
                for dx, dc in far:
                    for copy in direct_copies(dx, dc):
                        copy.wait_send()
        else:
            drain_far(j)
        for copy in kv_copies(0, 1, j):
            copy.wait_send()
        q_copy(j).wait_send()
        local, back = o_copies(j)
        local.wait()
        back.wait()

    @pl.when(helper)
    def _():
        for copy in across_copies() + back_copies(0):
            copy.wait_send()

    @pl.when(w_helper)
    def _():
        for x in range(chips):
            @pl.when(x != chip)
            def _():
                w_across(0, x).wait_send()

            @pl.when(jnp.logical_not(is_near(x)))
            def _():
                w_back(0, x).wait_send()

    @pl.when(last)
    def _():
        @pl.when(chip * 2 + w_side != me)
        def _():
            w_near().wait_send()

        for x in range(chips):
            @pl.when(x != chip)
            def _():
                w_direct(x).wait_send()
        for i in range(pieces - 1):
            for copy in out_copies(i):
                copy.wait_send()
        for c in range(comps):
            for side in range(2):
                if (c, side) != (comps - 1, 0):
                    noise_copy(c, side).wait_send()

    for side in range(2):
        pltpu.make_async_copy(nsend.at[0, side], nrecv.at[side], n_recv.at[side]).wait()
    total = nrecv[0] + nrecv[1]
    root = jnp.sqrt(total[pad:pad + 1] / width + 1e-06)
    noise_ref[...] = total[0:own] / root


def on_device(queries, keys, values, latent, prev_denoised, head_weight):
    n = lax.axis_size("seq")
    comps = lax.axis_size("comp")
    _, tokens, width = queries.shape
    half = width // 2
    own = latent.shape[0]
    channels = head_weight.shape[1]
    pad = -(-own // 8) * 8
    chips, rows_w = n // 2, width // n
    pieces = min(comps, tokens // 16)
    w_pieces = min(comps, rows_w // 128)
    bf16, f32 = jnp.bfloat16, jnp.float32
    dma = pltpu.SemaphoreType.DMA
    anywhere = pl.BlockSpec(memory_space=pl.ANY)
    hidden, noise_own = pl.pallas_call(
        functools.partial(kernel, n, comps, own),
        out_shape=(
            pltpu.VMEM((tokens, width), bf16),
            pltpu.VMEM((own, tokens), f32),
        ),
        in_specs=[anywhere] * 4,
        out_specs=(anywhere, pl.BlockSpec(memory_space=pltpu.VMEM)),
        scratch_shapes=[
            pltpu.VMEM((n, tokens, half), bf16),
            pltpu.VMEM((n, tokens, half), bf16),
            pltpu.VMEM((2, tokens, half), bf16),
            pltpu.VMEM((2, tokens, half), bf16),
            pltpu.VMEM((n // 2, channels, width // n), bf16),
            pltpu.VMEM((2 * tokens, channels), f32),
            pltpu.VMEM((2 * tokens, 1), f32),
            pltpu.VMEM((comps, 2, pad + 8, tokens), f32),
            pltpu.VMEM((2, pad + 8, tokens), f32),
            pltpu.VMEM((2, 2, tokens // pieces, SIZES[FINAL] * HD), bf16),
            pltpu.VMEM((n, 2, tokens // pieces, SIZES[FINAL] * HD), bf16),
            pltpu.VMEM((chips, channels, rows_w // w_pieces), bf16),
            dma((n, CHUNKS)), dma((n, CHUNKS)), dma((n, CHUNKS)), dma((n, CHUNKS)),
            dma((CHUNKS,)), dma((CHUNKS,)), dma((CHUNKS,)),
            dma((CHUNKS,)), dma((CHUNKS,)), dma((CHUNKS,)),
            dma((chips + 1,)), dma((chips,)),
            dma((comps, 2)), dma((2,)),
            dma((pieces, 2, 2)), dma((2, 2)), dma((n, 2)), dma((n, 2)), dma((n, 2)),
            dma((pieces, n, 2)),
            dma((chips,)), dma((chips,)), dma((chips,)), dma((w_pieces, chips)),
        ],
        compiler_params=pltpu.CompilerParams(
            collective_id=0, has_side_effects=True, vmem_limit_bytes=60 * 1024 * 1024
        ),
        name="attention_step",
    )(queries, keys, values, head_weight.T)
    denoised = (latent - sigma_now * noise_own) / alpha_now
    step_now = math.log(alpha_next / sigma_next) - math.log(alpha_now / sigma_now)
    ratio = step_before / step_now
    blend = (1.0 + 0.5 / ratio) * denoised - 0.5 / ratio * prev_denoised
    new_latent = sigma_next / sigma_now * latent - alpha_next * (math.exp(-step_now) - 1.0) * blend
    return (hidden[None], new_latent, denoised)


def solution(mesh):
    return jax.shard_map(
        on_device,
        mesh=mesh,
        in_specs=(
            P("comp", "seq", None),
            P("comp", "seq", None),
            P("comp", "seq", None),
            P("comp", "seq"),
            P("comp", "seq"),
            P("seq", None),
        ),
        out_specs=(P("comp", "seq", None), P("comp", "seq"), P("comp", "seq")),
        check_vma=False,
    )
```

```python
import functools
import math

import jax
import jax.numpy as jnp
from jax import lax
from jax.experimental import pallas as pl
from jax.experimental.pallas import tpu as pltpu
from jax.sharding import PartitionSpec as P

HD = 128
SIZES = (4, 4, 4, 2, 1, 1)
CHUNKS = len(SIZES)
FIRST = tuple(sum(SIZES[:j]) for j in range(CHUNKS))
FINAL = 3
LATE = 2
STARTS = {0: (2,), 1: (3,), 2: (4, 5)}
MESH = pl.DeviceIdType.MESH

alpha_now = 0.6
sigma_now = 0.8
alpha_next = 0.8
sigma_next = 0.6
step_before = 0.4


def kernel(
    n, comps, own, q_hbm, k_hbm, v_hbm, w_hbm, hid_hbm, noise_ref,
    kbuf, vbuf, qbuf, obuf, wbuf, acc, sq, nsend, nrecv, relay_in, relay_mid, w_mid,
    k_send, k_recv, v_send, v_recv, q_send, q_recv, q_local,
    o_send, o_recv, o_local, w_send, w_recv, n_send, n_recv,
    in_send, in_recv, mid_send, mid_recv, back_send, piece_recv,
    wm_send, wm_recv, wb_send, w_piece,
):
    tokens, width = hid_hbm.shape
    half = width // 2
    chips = n // 2
    assert sum(SIZES) * HD == half
    rows_w = width // n
    pad = nsend.shape[2] - 8
    comp = lax.axis_index("comp")
    me = lax.axis_index("seq")
    chip, core = me // 2, me % 2
    mate = chip * 2 + 1 - core
    last = comp == comps - 1

    def peer(d_chip, d_core):
        return lax.rem(chip + d_chip, chips) * 2 + lax.rem(core + d_core, 2)

    barrier = pltpu.get_barrier_semaphore()
    others = [(dx, dc) for dx in range(chips) for dc in range(2) if (dx, dc) != (0, 0)]
    for dx, dc in others:
        pl.semaphore_signal(barrier, inc=1, device_id=(comp, peer(dx, dc)), device_id_type=MESH)

    @pl.when(jnp.logical_not(last))
    def _():
        for target in (me, mate):
            pl.semaphore_signal(
                barrier, inc=1, device_id=(comps - 1, target), device_id_type=MESH
            )
        pl.semaphore_wait(barrier, n - 1)

    @pl.when(last)
    def _():
        pl.semaphore_wait(barrier, n - 1 + 2 * (comps - 1))

    pieces, piece_rows = piece_recv.shape[0], relay_in.shape[2]
    w_pieces, piece_cols = w_piece.shape[0], w_mid.shape[2]
    helper = jnp.logical_and(jnp.logical_not(last), comp >= comps - pieces)
    w_helper = jnp.logical_and(jnp.logical_not(last), comp >= comps - w_pieces)
    final = FINAL
    far = [(dx, dc) for dx in range(1, chips) for dc in range(2)]
    far_slots = [((chips - dx) % chips) * 2 + dc for dx, dc in far]

    def columns(side, j):
        start = pl.multiple_of(side * half + FIRST[j] * HD, HD)
        return pl.ds(start, SIZES[j] * HD)

    def kept(j):
        return pl.ds(FIRST[j] * HD, SIZES[j] * HD)

    def remote(src, dst, send, recv, target, owner=comp):
        return pltpu.make_async_remote_copy(
            src_ref=src, dst_ref=dst, send_sem=send, recv_sem=recv,
            device_id=(owner, target), device_id_type=MESH,
        )

    def kv_copies(dx, dc, j):
        target = peer(dx, dc)
        side = lax.rem(core + dc, 2)
        slot = ((chips - dx) % chips) * 2 + dc
        return [
            remote(src.at[0, :, columns(side, j)], buf.at[slot, :, kept(j)],
                   send.at[slot, j], recv.at[slot, j], target)
            for src, buf, send, recv in (
                (k_hbm, kbuf, k_send, k_recv), (v_hbm, vbuf, v_send, v_recv))
        ]

    def q_copy(j):
        return remote(q_hbm.at[0, :, columns(1 - core, j)], qbuf.at[1, :, kept(j)],
                      q_send.at[j], q_recv.at[j], mate)

    def local_copies(j):
        mine = columns(core, j)
        return [
            pltpu.make_async_copy(q_hbm.at[0, :, mine], qbuf.at[0, :, kept(j)], q_local.at[j]),
            pltpu.make_async_copy(k_hbm.at[0, :, mine], kbuf.at[0, :, kept(j)], k_recv.at[0, j]),
            pltpu.make_async_copy(v_hbm.at[0, :, mine], vbuf.at[0, :, kept(j)], v_recv.at[0, j]),
        ]

    def o_copies(j):
        mine = columns(core, j)
        return [
            pltpu.make_async_copy(obuf.at[0, :, kept(j)], hid_hbm.at[:, mine], o_local.at[j]),
            remote(obuf.at[1, :, kept(j)], hid_hbm.at[:, mine], o_send.at[j], o_recv.at[j], mate),
        ]

    def piece(i):
        return pl.ds(i * piece_rows, piece_rows)

    def direct_copies(dx, dc):
        slot = ((chips - dx) % chips) * 2 + dc
        side = lax.rem(core + dc, 2)
        return [
            remote(src.at[0, piece(pieces - 1), columns(side, final)],
                   buf.at[slot, piece(pieces - 1), kept(final)],
                   send.at[slot, final], piece_recv.at[pieces - 1, slot, kind], peer(dx, dc))
            for kind, (src, buf, send) in enumerate(
                ((k_hbm, kbuf, k_send), (v_hbm, vbuf, v_send)))
        ]

    def out_copies(i):
        return [
            remote(src.at[0, piece(i), columns(side, final)], relay_in.at[kind, side],
                   in_send.at[i, kind, side], in_recv.at[kind, side],
                   me, comps - pieces + i)
            for kind, src in enumerate((k_hbm, v_hbm)) for side in range(2)
        ]

    def across_copies():
        copies = []
        for (dx, dc), slot in zip(far, far_slots):
            for kind in range(2):
                copies.append(remote(
                    relay_in.at[kind, lax.rem(core + dc, 2)], relay_mid.at[slot, kind],
                    mid_send.at[slot, kind], mid_recv.at[slot, kind], peer(dx, dc)))
        return copies

    def back_copies(i):
        return [
            remote(relay_mid.at[slot, kind], buf.at[slot, piece(i), kept(final)],
                   back_send.at[slot, kind], piece_recv.at[i, slot, kind], me, comps - 1)
            for slot in far_slots for kind, buf in enumerate((kbuf, vbuf))
        ]

    def piece_arrivals(i):
        return [
            pltpu.make_async_copy(buf.at[slot, piece(i), kept(final)],
                                  buf.at[slot, piece(i), kept(final)],
                                  piece_recv.at[i, slot, kind])
            for slot in far_slots for kind, buf in enumerate((kbuf, vbuf))
        ]

    w_side = me // chips
    w_slot = lax.rem(me, chips)

    def w_cols(i):
        return pl.ds(i * piece_cols, piece_cols)

    def w_near():
        return remote(w_hbm, wbuf.at[w_slot], w_send.at[chips], w_recv.at[w_slot],
                      chip * 2 + w_side)

    def w_direct(x):
        return remote(w_hbm.at[:, w_cols(w_pieces - 1)], wbuf.at[w_slot, :, w_cols(w_pieces - 1)],
                      w_send.at[x], w_piece.at[w_pieces - 1, w_slot], x * 2 + w_side)

    def w_across(i, x):
        return remote(w_hbm.at[:, w_cols(i)], w_mid.at[w_slot],
                      wm_send.at[x], wm_recv.at[w_slot], x * 2 + w_side)

    def w_back(i, x):
        return remote(w_mid.at[x], wbuf.at[x, :, w_cols(i)],
                      wb_send.at[x], w_piece.at[i, x], me, comps - 1)

    def is_near(slot):
        return (core * chips + slot) // 2 == chip

    @pl.when(last)
    def _():
        @pl.when(chip * 2 + w_side != me)
        def _():
            w_near().start()

        @pl.when(chip * 2 + w_side == me)
        def _():
            pltpu.make_async_copy(w_hbm, wbuf.at[w_slot], w_recv.at[w_slot]).start()

        for x in range(chips):
            @pl.when(x != chip)
            def _():
                w_direct(x).start()

        acc[...] = jnp.zeros_like(acc)
        sq[...] = jnp.zeros_like(sq)

    for i in range(w_pieces - 1):
        @pl.when(comp == comps - w_pieces + i)
        def _():
            for x in range(chips):
                @pl.when(x != chip)
                def _():
                    w_across(i, x).start()

    def start_far(j):
        for dx, dc in far:
            for copy in kv_copies(dx, dc, j):
                copy.start()

    def start_chunk(j):
        if j == final:
            @pl.when(jnp.logical_not(last))
            def _():
                start_far(j)

            @pl.when(last)
            def _():
                for dx, dc in far:
                    for copy in direct_copies(dx, dc):
                        copy.start()
        else:
            start_far(j)
        for copy in kv_copies(0, 1, j):
            copy.start()
        q_copy(j).start()
        for copy in local_copies(j):
            copy.start()

    start_chunk(0)
    start_chunk(1)

    @pl.when(last)
    def _():
        for i in range(pieces - 1):
            for copy in out_copies(i):
                copy.start()

    def relay_across():
        @pl.when(helper)
        def _():
            for copy in out_copies(0):
                copy.wait_recv()
            for copy in across_copies():
                copy.start()

    def relay_back():
        @pl.when(helper)
        def _():
            for copy in across_copies():
                copy.wait_recv()
        for i in range(pieces - 1):
            @pl.when(comp == comps - pieces + i)
            def _():
                for copy in back_copies(i):
                    copy.start()
        for i in range(w_pieces - 1):
            @pl.when(comp == comps - w_pieces + i)
            def _():
                for x in range(chips):
                    @pl.when(jnp.logical_not(is_near(x)))
                    def _():
                        pltpu.make_async_copy(w_mid.at[x], w_mid.at[x], wm_recv.at[x]).wait()
                        w_back(i, x).start()

    def await_rows():
        for x in range(chips):
            @pl.when(is_near(x))
            def _():
                pltpu.make_async_copy(wbuf.at[x], wbuf.at[x], w_recv.at[x]).wait()

            @pl.when(jnp.logical_not(is_near(x)))
            def _():
                for i in range(w_pieces):
                    dst = wbuf.at[x, :, w_cols(i)]
                    pltpu.make_async_copy(dst, dst, w_piece.at[i, x]).wait()

    def project(j):
        unit = min(SIZES[j], 2) * HD
        for first in range(FIRST[j] * HD, (FIRST[j] + SIZES[j]) * HD, unit):
            part = obuf[:, :, first:first + unit].reshape(2 * tokens, unit)
            at = first % rows_w
            rows = wbuf[first // rows_w, :, at:at + unit]
            acc[...] += lax.dot_general(
                part, rows, (((1,), (1,)), ((), ())), preferred_element_type=jnp.float32
            )
            wide = part.astype(jnp.float32)
            sq[...] += jnp.sum(wide * wide, axis=1, keepdims=True)

    factor = HD ** (-0.5) * math.log2(math.e)

    def wait_far(j):
        for dx, dc in far:
            for copy in kv_copies(dx, dc, j):
                copy.wait_recv()

    def attend(j):
        for copy in local_copies(j):
            copy.wait()
        q_copy(j).wait_recv()
        for copy in kv_copies(0, 1, j):
            copy.wait_recv()
        if j == final:
            @pl.when(jnp.logical_not(last))
            def _():
                wait_far(j)

            @pl.when(last)
            def _():
                for i in range(pieces):
                    for copy in piece_arrivals(i):
                        copy.wait()
        else:
            wait_far(j)

        if j == 0:
            relay_across()
        if j == 1:
            relay_back()
        for later in STARTS.get(j, ()):
            start_chunk(later)

        step = min(SIZES[j], 2)

        def heads(turn, carry):
            for h in range(step):
                at = (FIRST[j] + turn * step + h) * HD
                cols = pl.ds(pl.multiple_of(at, HD), HD)
                query = qbuf[:, :, cols].reshape(2 * tokens, HD)
                key = kbuf[:, :, cols].reshape(n * tokens, HD)
                value = vbuf[:, :, cols].reshape(n * tokens, HD)
                scores = lax.dot_general(
                    query, key, (((1,), (1,)), ((), ())), preferred_element_type=jnp.float32
                )
                highest = jnp.max(scores, axis=1, keepdims=True)
                weights = jnp.exp2((scores - highest) * factor)
                wide = jnp.concatenate([value, jnp.ones_like(value)], axis=1)
                out = jnp.dot(
                    weights.astype(jnp.bfloat16), wide, preferred_element_type=jnp.float32
                )
                out = (out[:, :HD] / out[:, HD:]).astype(jnp.bfloat16)
                obuf[:, :, cols] = out.reshape(2, tokens, HD)
            return carry

        lax.fori_loop(0, SIZES[j] // step, heads, 0)
        for copy in o_copies(j):
            copy.start()

        if j >= LATE:
            @pl.when(last)
            def _():
                if j == LATE:
                    await_rows()
                for done in range(0 if j == LATE else j, j + 1):
                    project(done)

    for j in range(CHUNKS):
        attend(j)

    def noise_copy(c, side):
        return pltpu.make_async_remote_copy(
            src_ref=nsend.at[c, side], dst_ref=nrecv.at[side],
            send_sem=n_send.at[c, side], recv_sem=n_recv.at[side],
            device_id=(c, me if side == 0 else mate), device_id_type=MESH,
        )

    def noise_self():
        return pltpu.make_async_copy(nsend.at[comps - 1, 0], nrecv.at[0], n_recv.at[0])

    @pl.when(last)
    def _():
        both = jnp.concatenate([acc[...], jnp.broadcast_to(sq[...], acc.shape)], axis=1).T
        channels = acc.shape[1]
        for c in range(comps):
            for side in range(2):
                toks = slice(side * tokens, (side + 1) * tokens)
                nsend[c, side, 0:own, :] = both[c * own:(c + 1) * own, toks]
                nsend[c, side, pad:pad + 8, :] = both[channels:channels + 8, toks]
        for c in range(comps):
            for side in range(2):
                if (c, side) == (comps - 1, 0):
                    noise_self().start()
                else:
                    noise_copy(c, side).start()

    def drain_far(j):
        for dx, dc in far:
            for copy in kv_copies(dx, dc, j):
                copy.wait_send()

    for j in range(CHUNKS):
        if j == final:
            @pl.when(jnp.logical_not(last))
            def _():
                drain_far(final)

            @pl.when(last)
            def _():
                for dx, dc in far:
                    for copy in direct_copies(dx, dc):
                        copy.wait_send()
        else:
            drain_far(j)
        for copy in kv_copies(0, 1, j):
            copy.wait_send()
        q_copy(j).wait_send()
        local, back = o_copies(j)
        local.wait()
        back.wait()

    @pl.when(helper)
    def _():
        for copy in across_copies() + back_copies(0):
            copy.wait_send()

    @pl.when(w_helper)
    def _():
        for x in range(chips):
            @pl.when(x != chip)
            def _():
                w_across(0, x).wait_send()

            @pl.when(jnp.logical_not(is_near(x)))
            def _():
                w_back(0, x).wait_send()

    @pl.when(last)
    def _():
        @pl.when(chip * 2 + w_side != me)
        def _():
            w_near().wait_send()

        for x in range(chips):
            @pl.when(x != chip)
            def _():
                w_direct(x).wait_send()
        for i in range(pieces - 1):
            for copy in out_copies(i):
                copy.wait_send()
        for c in range(comps):
            for side in range(2):
                if (c, side) != (comps - 1, 0):
                    noise_copy(c, side).wait_send()

    for side in range(2):
        pltpu.make_async_copy(nsend.at[0, side], nrecv.at[side], n_recv.at[side]).wait()
    total = nrecv[0] + nrecv[1]
    root = jnp.sqrt(total[pad:pad + 1] / width + 1e-06)
    noise_ref[...] = total[0:own] / root


def on_device(queries, keys, values, latent, prev_denoised, head_weight):
    n = lax.axis_size("seq")
    comps = lax.axis_size("comp")
    _, tokens, width = queries.shape
    half = width // 2
    own = latent.shape[0]
    channels = head_weight.shape[1]
    pad = -(-own // 8) * 8
    chips, rows_w = n // 2, width // n
    pieces = min(comps, tokens // 16)
    w_pieces = min(comps, rows_w // 128)
    bf16, f32 = jnp.bfloat16, jnp.float32
    dma = pltpu.SemaphoreType.DMA
    anywhere = pl.BlockSpec(memory_space=pl.ANY)
    hidden, noise_own = pl.pallas_call(
        functools.partial(kernel, n, comps, own),
        out_shape=(
            pltpu.VMEM((tokens, width), bf16),
            pltpu.VMEM((own, tokens), f32),
        ),
        in_specs=[anywhere] * 4,
        out_specs=(anywhere, pl.BlockSpec(memory_space=pltpu.VMEM)),
        scratch_shapes=[
            pltpu.VMEM((n, tokens, half), bf16),
            pltpu.VMEM((n, tokens, half), bf16),
            pltpu.VMEM((2, tokens, half), bf16),
            pltpu.VMEM((2, tokens, half), bf16),
            pltpu.VMEM((n // 2, channels, width // n), bf16),
            pltpu.VMEM((2 * tokens, channels), f32),
            pltpu.VMEM((2 * tokens, 1), f32),
            pltpu.VMEM((comps, 2, pad + 8, tokens), f32),
            pltpu.VMEM((2, pad + 8, tokens), f32),
            pltpu.VMEM((2, 2, tokens // pieces, SIZES[FINAL] * HD), bf16),
            pltpu.VMEM((n, 2, tokens // pieces, SIZES[FINAL] * HD), bf16),
            pltpu.VMEM((chips, channels, rows_w // w_pieces), bf16),
            dma((n, CHUNKS)), dma((n, CHUNKS)), dma((n, CHUNKS)), dma((n, CHUNKS)),
            dma((CHUNKS,)), dma((CHUNKS,)), dma((CHUNKS,)),
            dma((CHUNKS,)), dma((CHUNKS,)), dma((CHUNKS,)),
            dma((chips + 1,)), dma((chips,)),
            dma((comps, 2)), dma((2,)),
            dma((pieces, 2, 2)), dma((2, 2)), dma((n, 2)), dma((n, 2)), dma((n, 2)),
            dma((pieces, n, 2)),
            dma((chips,)), dma((chips,)), dma((chips,)), dma((w_pieces, chips)),
        ],
        compiler_params=pltpu.CompilerParams(
            collective_id=0, has_side_effects=True, vmem_limit_bytes=60 * 1024 * 1024
        ),
        name="attention_step",
    )(queries, keys, values, head_weight.T)
    denoised = (latent - sigma_now * noise_own) / alpha_now
    step_now = math.log(alpha_next / sigma_next) - math.log(alpha_now / sigma_now)
    ratio = step_before / step_now
    blend = (1.0 + 0.5 / ratio) * denoised - 0.5 / ratio * prev_denoised
    new_latent = sigma_next / sigma_now * latent - alpha_next * (math.exp(-step_now) - 1.0) * blend
    return (hidden[None], new_latent, denoised)


def solution(mesh):
    return jax.shard_map(
        on_device,
        mesh=mesh,
        in_specs=(
            P("comp", "seq", None),
            P("comp", "seq", None),
            P("comp", "seq", None),
            P("comp", "seq"),
            P("comp", "seq"),
            P("seq", None),
        ),
        out_specs=(P("comp", "seq", None), P("comp", "seq"), P("comp", "seq")),
        check_vma=False,
    )
```

```python
import functools
import math

import jax
import jax.numpy as jnp
from jax import lax
from jax.experimental import pallas as pl
from jax.experimental.pallas import tpu as pltpu
from jax.sharding import PartitionSpec as P

HD = 128
CHUNKS = 8
WINDOW = 2
LATE = 5
MESH = pl.DeviceIdType.MESH

alpha_now = 0.6
sigma_now = 0.8
alpha_next = 0.8
sigma_next = 0.6
step_before = 0.4


def kernel(
    n, comps, own, q_hbm, k_hbm, v_hbm, w_hbm, hid_hbm, noise_ref,
    kbuf, vbuf, qbuf, obuf, wbuf, acc, sq, nsend, nrecv, relay_in, relay_mid, w_mid,
    k_send, k_recv, v_send, v_recv, q_send, q_recv, q_local,
    o_send, o_recv, o_local, w_send, w_recv, n_send, n_recv,
    in_send, in_recv, mid_send, mid_recv, back_send, piece_recv,
    wm_send, wm_recv, wb_send, w_piece,
):
    tokens, width = hid_hbm.shape
    half = width // 2
    chips = n // 2
    cw = half // CHUNKS
    rows_w = width // n
    pad = nsend.shape[2] - 8
    comp = lax.axis_index("comp")
    me = lax.axis_index("seq")
    chip, core = me // 2, me % 2
    mate = chip * 2 + 1 - core
    last = comp == comps - 1

    def peer(d_chip, d_core):
        return lax.rem(chip + d_chip, chips) * 2 + lax.rem(core + d_core, 2)

    barrier = pltpu.get_barrier_semaphore()
    others = [(dx, dc) for dx in range(chips) for dc in range(2) if (dx, dc) != (0, 0)]
    for dx, dc in others:
        pl.semaphore_signal(barrier, inc=1, device_id=(comp, peer(dx, dc)), device_id_type=MESH)

    @pl.when(jnp.logical_not(last))
    def _():
        for target in (me, mate):
            pl.semaphore_signal(
                barrier, inc=1, device_id=(comps - 1, target), device_id_type=MESH
            )
        pl.semaphore_wait(barrier, n - 1)

    @pl.when(last)
    def _():
        pl.semaphore_wait(barrier, n - 1 + 2 * (comps - 1))

    pieces, piece_rows = piece_recv.shape[0], relay_in.shape[2]
    w_pieces, piece_cols = w_piece.shape[0], w_mid.shape[2]
    helper = jnp.logical_and(jnp.logical_not(last), comp >= comps - pieces)
    w_helper = jnp.logical_and(jnp.logical_not(last), comp >= comps - w_pieces)
    final = CHUNKS - 1
    far = [(dx, dc) for dx in range(1, chips) for dc in range(2)]
    far_slots = [((chips - dx) % chips) * 2 + dc for dx, dc in far]

    def columns(side, j):
        return pl.ds(pl.multiple_of(side * half + j * cw, cw), cw)

    def kept(j):
        return pl.ds(pl.multiple_of(j * cw, cw), cw)

    def remote(src, dst, send, recv, target, owner=comp):
        return pltpu.make_async_remote_copy(
            src_ref=src, dst_ref=dst, send_sem=send, recv_sem=recv,
            device_id=(owner, target), device_id_type=MESH,
        )

    def kv_copies(dx, dc, j):
        target = peer(dx, dc)
        side = lax.rem(core + dc, 2)
        slot = ((chips - dx) % chips) * 2 + dc
        return [
            remote(src.at[0, :, columns(side, j)], buf.at[slot, :, kept(j)],
                   send.at[slot, j], recv.at[slot, j], target)
            for src, buf, send, recv in (
                (k_hbm, kbuf, k_send, k_recv), (v_hbm, vbuf, v_send, v_recv))
        ]

    def q_copy(j):
        return remote(q_hbm.at[0, :, columns(1 - core, j)], qbuf.at[1, :, kept(j)],
                      q_send.at[j], q_recv.at[j], mate)

    def local_copies(j):
        mine = columns(core, j)
        return [
            pltpu.make_async_copy(q_hbm.at[0, :, mine], qbuf.at[0, :, kept(j)], q_local.at[j]),
            pltpu.make_async_copy(k_hbm.at[0, :, mine], kbuf.at[0, :, kept(j)], k_recv.at[0, j]),
            pltpu.make_async_copy(v_hbm.at[0, :, mine], vbuf.at[0, :, kept(j)], v_recv.at[0, j]),
        ]

    def o_copies(j):
        mine = columns(core, j)
        return [
            pltpu.make_async_copy(obuf.at[0, :, kept(j)], hid_hbm.at[:, mine], o_local.at[j]),
            remote(obuf.at[1, :, kept(j)], hid_hbm.at[:, mine], o_send.at[j], o_recv.at[j], mate),
        ]

    def piece(i):
        return pl.ds(i * piece_rows, piece_rows)

    def direct_copies(dx, dc):
        slot = ((chips - dx) % chips) * 2 + dc
        side = lax.rem(core + dc, 2)
        return [
            remote(src.at[0, piece(pieces - 1), columns(side, final)],
                   buf.at[slot, piece(pieces - 1), kept(final)],
                   send.at[slot, final], piece_recv.at[pieces - 1, slot, kind], peer(dx, dc))
            for kind, (src, buf, send) in enumerate(
                ((k_hbm, kbuf, k_send), (v_hbm, vbuf, v_send)))
        ]

    def out_copies(i):
        return [
            remote(src.at[0, piece(i), columns(side, final)], relay_in.at[kind, side],
                   in_send.at[i, kind, side], in_recv.at[kind, side],
                   me, comps - pieces + i)
            for kind, src in enumerate((k_hbm, v_hbm)) for side in range(2)
        ]

    def across_copies():
        copies = []
        for (dx, dc), slot in zip(far, far_slots):
            for kind in range(2):
                copies.append(remote(
                    relay_in.at[kind, lax.rem(core + dc, 2)], relay_mid.at[slot, kind],
                    mid_send.at[slot, kind], mid_recv.at[slot, kind], peer(dx, dc)))
        return copies

    def back_copies(i):
        return [
            remote(relay_mid.at[slot, kind], buf.at[slot, piece(i), kept(final)],
                   back_send.at[slot, kind], piece_recv.at[i, slot, kind], me, comps - 1)
            for slot in far_slots for kind, buf in enumerate((kbuf, vbuf))
        ]

    def piece_arrivals(i):
        return [
            pltpu.make_async_copy(buf.at[slot, piece(i), kept(final)],
                                  buf.at[slot, piece(i), kept(final)],
                                  piece_recv.at[i, slot, kind])
            for slot in far_slots for kind, buf in enumerate((kbuf, vbuf))
        ]

    w_side = me // chips
    w_slot = lax.rem(me, chips)

    def w_cols(i):
        return pl.ds(i * piece_cols, piece_cols)

    def w_near():
        return remote(w_hbm, wbuf.at[w_slot], w_send.at[chips], w_recv.at[w_slot],
                      chip * 2 + w_side)

    def w_direct(x):
        return remote(w_hbm.at[:, w_cols(w_pieces - 1)], wbuf.at[w_slot, :, w_cols(w_pieces - 1)],
                      w_send.at[x], w_piece.at[w_pieces - 1, w_slot], x * 2 + w_side)

    def w_across(i, x):
        return remote(w_hbm.at[:, w_cols(i)], w_mid.at[w_slot],
                      wm_send.at[x], wm_recv.at[w_slot], x * 2 + w_side)

    def w_back(i, x):
        return remote(w_mid.at[x], wbuf.at[x, :, w_cols(i)],
                      wb_send.at[x], w_piece.at[i, x], me, comps - 1)

    def is_near(slot):
        return (core * chips + slot) // 2 == chip

    @pl.when(last)
    def _():
        @pl.when(chip * 2 + w_side != me)
        def _():
            w_near().start()

        @pl.when(chip * 2 + w_side == me)
        def _():
            pltpu.make_async_copy(w_hbm, wbuf.at[w_slot], w_recv.at[w_slot]).start()

        for x in range(chips):
            @pl.when(x != chip)
            def _():
                w_direct(x).start()

        acc[...] = jnp.zeros_like(acc)
        sq[...] = jnp.zeros_like(sq)

    for i in range(w_pieces - 1):
        @pl.when(comp == comps - w_pieces + i)
        def _():
            for x in range(chips):
                @pl.when(x != chip)
                def _():
                    w_across(i, x).start()

    def start_chunk(j, carry):
        cut = jnp.logical_and(last, j == final)

        def start_mate():
            for copy in kv_copies(0, 1, j):
                copy.start()
            q_copy(j).start()

        pl.when(core == 1)(start_mate)

        @pl.when(jnp.logical_not(cut))
        def _():
            for dx, dc in far:
                for copy in kv_copies(dx, dc, j):
                    copy.start()

        @pl.when(cut)
        def _():
            for dx, dc in far:
                for copy in direct_copies(dx, dc):
                    copy.start()

        pl.when(core == 0)(start_mate)
        for copy in local_copies(j):
            copy.start()
        return carry

    lax.fori_loop(0, WINDOW, start_chunk, 0)

    @pl.when(last)
    def _():
        for i in range(pieces - 1):
            for copy in out_copies(i):
                copy.start()

    def relay_across():
        @pl.when(helper)
        def _():
            for copy in out_copies(0):
                copy.wait_recv()
            for copy in across_copies():
                copy.start()

    def relay_back():
        @pl.when(helper)
        def _():
            for copy in across_copies():
                copy.wait_recv()
        for i in range(pieces - 1):
            @pl.when(comp == comps - pieces + i)
            def _():
                for copy in back_copies(i):
                    copy.start()
        for i in range(w_pieces - 1):
            @pl.when(comp == comps - w_pieces + i)
            def _():
                for x in range(chips):
                    @pl.when(jnp.logical_not(is_near(x)))
                    def _():
                        pltpu.make_async_copy(w_mid.at[x], w_mid.at[x], wm_recv.at[x]).wait()
                        w_back(i, x).start()

    def await_rows():
        for x in range(chips):
            @pl.when(is_near(x))
            def _():
                pltpu.make_async_copy(wbuf.at[x], wbuf.at[x], w_recv.at[x]).wait()

            @pl.when(jnp.logical_not(is_near(x)))
            def _():
                for i in range(w_pieces):
                    dst = wbuf.at[x, :, w_cols(i)]
                    pltpu.make_async_copy(dst, dst, w_piece.at[i, x]).wait()

    def project(j, carry):
        part = obuf[:, :, kept(j)].reshape(2 * tokens, cw)
        first = j * cw
        rows = wbuf[first // rows_w, :, pl.ds(pl.multiple_of(first % rows_w, cw), cw)]
        acc[...] += lax.dot_general(
            part, rows, (((1,), (1,)), ((), ())), preferred_element_type=jnp.float32
        )
        wide = part.astype(jnp.float32)
        sq[...] += jnp.sum(wide * wide, axis=1, keepdims=True)
        return carry

    factor = HD ** (-0.5) * math.log2(math.e)

    def attend(j, carry):
        for copy in local_copies(j):
            copy.wait()
        q_copy(j).wait_recv()
        for copy in kv_copies(0, 1, j):
            copy.wait_recv()
        cut = jnp.logical_and(last, j == final)

        @pl.when(jnp.logical_not(cut))
        def _():
            for dx, dc in far:
                for copy in kv_copies(dx, dc, j):
                    copy.wait_recv()

        @pl.when(cut)
        def _():
            for i in range(pieces):
                for copy in piece_arrivals(i):
                    copy.wait()

        pl.when(j == 1)(relay_across)
        pl.when(j == 3)(relay_back)

        @pl.when(j + WINDOW < CHUNKS)
        def _():
            start_chunk(j + WINDOW, 0)

        for h in range(cw // HD):
            cols = pl.ds(pl.multiple_of(j * cw + h * HD, HD), HD)
            query = qbuf[:, :, cols].reshape(2 * tokens, HD)
            key = kbuf[:, :, cols].reshape(n * tokens, HD)
            value = vbuf[:, :, cols].reshape(n * tokens, HD)
            scores = lax.dot_general(
                query, key, (((1,), (1,)), ((), ())), preferred_element_type=jnp.float32
            )
            highest = jnp.max(scores, axis=1, keepdims=True)
            weights = jnp.exp2((scores - highest) * factor)
            totals = jnp.sum(weights, axis=1, keepdims=True)
            out = jnp.dot(weights.astype(jnp.bfloat16), value, preferred_element_type=jnp.float32)
            out = (out / totals).astype(jnp.bfloat16)
            obuf[:, :, cols] = out.reshape(2, tokens, HD)
        for copy in o_copies(j):
            copy.start()

        @pl.when(jnp.logical_and(last, j == LATE))
        def _():
            await_rows()
            lax.fori_loop(0, LATE + 1, project, 0)

        @pl.when(jnp.logical_and(last, j > LATE))
        def _():
            project(j, 0)

        return carry

    lax.fori_loop(0, CHUNKS, attend, 0)

    def noise_copy(c, side):
        return pltpu.make_async_remote_copy(
            src_ref=nsend.at[c, side], dst_ref=nrecv.at[side],
            send_sem=n_send.at[c, side], recv_sem=n_recv.at[side],
            device_id=(c, me if side == 0 else mate), device_id_type=MESH,
        )

    def noise_self():
        return pltpu.make_async_copy(nsend.at[comps - 1, 0], nrecv.at[0], n_recv.at[0])

    @pl.when(last)
    def _():
        both = jnp.concatenate([acc[...], jnp.broadcast_to(sq[...], acc.shape)], axis=1).T
        channels = acc.shape[1]
        for c in range(comps):
            for side in range(2):
                toks = slice(side * tokens, (side + 1) * tokens)
                nsend[c, side, 0:own, :] = both[c * own:(c + 1) * own, toks]
                nsend[c, side, pad:pad + 8, :] = both[channels:channels + 8, toks]
        for c in range(comps):
            for side in range(2):
                if (c, side) == (comps - 1, 0):
                    noise_self().start()
                else:
                    noise_copy(c, side).start()

    def drain(j, carry):
        cut = jnp.logical_and(last, j == final)

        @pl.when(jnp.logical_not(cut))
        def _():
            for dx, dc in far:
                for copy in kv_copies(dx, dc, j):
                    copy.wait_send()

        @pl.when(cut)
        def _():
            for dx, dc in far:
                for copy in direct_copies(dx, dc):
                    copy.wait_send()

        for copy in kv_copies(0, 1, j):
            copy.wait_send()
        q_copy(j).wait_send()
        local, back = o_copies(j)
        local.wait()
        back.wait()
        return carry

    lax.fori_loop(0, CHUNKS, drain, 0)

    @pl.when(helper)
    def _():
        for copy in across_copies() + back_copies(0):
            copy.wait_send()

    @pl.when(w_helper)
    def _():
        for x in range(chips):
            @pl.when(x != chip)
            def _():
                w_across(0, x).wait_send()

            @pl.when(jnp.logical_not(is_near(x)))
            def _():
                w_back(0, x).wait_send()

    @pl.when(last)
    def _():
        @pl.when(chip * 2 + w_side != me)
        def _():
            w_near().wait_send()

        for x in range(chips):
            @pl.when(x != chip)
            def _():
                w_direct(x).wait_send()
        for i in range(pieces - 1):
            for copy in out_copies(i):
                copy.wait_send()
        for c in range(comps):
            for side in range(2):
                if (c, side) != (comps - 1, 0):
                    noise_copy(c, side).wait_send()

    for side in range(2):
        pltpu.make_async_copy(nsend.at[0, side], nrecv.at[side], n_recv.at[side]).wait()
    total = nrecv[0] + nrecv[1]
    root = jnp.sqrt(total[pad:pad + 1] / width + 1e-06)
    noise_ref[...] = total[0:own] / root


def on_device(queries, keys, values, latent, prev_denoised, head_weight):
    n = lax.axis_size("seq")
    comps = lax.axis_size("comp")
    _, tokens, width = queries.shape
    half = width // 2
    own = latent.shape[0]
    channels = head_weight.shape[1]
    pad = -(-own // 8) * 8
    chips, rows_w = n // 2, width // n
    pieces = min(comps, tokens // 16)
    w_pieces = min(comps, rows_w // 128)
    bf16, f32 = jnp.bfloat16, jnp.float32
    dma = pltpu.SemaphoreType.DMA
    anywhere = pl.BlockSpec(memory_space=pl.ANY)
    hidden, noise_own = pl.pallas_call(
        functools.partial(kernel, n, comps, own),
        out_shape=(
            pltpu.VMEM((tokens, width), bf16),
            pltpu.VMEM((own, tokens), f32),
        ),
        in_specs=[anywhere] * 4,
        out_specs=(anywhere, pl.BlockSpec(memory_space=pltpu.VMEM)),
        scratch_shapes=[
            pltpu.VMEM((n, tokens, half), bf16),
            pltpu.VMEM((n, tokens, half), bf16),
            pltpu.VMEM((2, tokens, half), bf16),
            pltpu.VMEM((2, tokens, half), bf16),
            pltpu.VMEM((n // 2, channels, width // n), bf16),
            pltpu.VMEM((2 * tokens, channels), f32),
            pltpu.VMEM((2 * tokens, 1), f32),
            pltpu.VMEM((comps, 2, pad + 8, tokens), f32),
            pltpu.VMEM((2, pad + 8, tokens), f32),
            pltpu.VMEM((2, 2, tokens // pieces, half // CHUNKS), bf16),
            pltpu.VMEM((n, 2, tokens // pieces, half // CHUNKS), bf16),
            pltpu.VMEM((chips, channels, rows_w // w_pieces), bf16),
            dma((n, CHUNKS)), dma((n, CHUNKS)), dma((n, CHUNKS)), dma((n, CHUNKS)),
            dma((CHUNKS,)), dma((CHUNKS,)), dma((CHUNKS,)),
            dma((CHUNKS,)), dma((CHUNKS,)), dma((CHUNKS,)),
            dma((chips + 1,)), dma((chips,)),
            dma((comps, 2)), dma((2,)),
            dma((pieces, 2, 2)), dma((2, 2)), dma((n, 2)), dma((n, 2)), dma((n, 2)),
            dma((pieces, n, 2)),
            dma((chips,)), dma((chips,)), dma((chips,)), dma((w_pieces, chips)),
        ],
        compiler_params=pltpu.CompilerParams(
            collective_id=0, has_side_effects=True, vmem_limit_bytes=60 * 1024 * 1024
        ),
        name="attention_step",
    )(queries, keys, values, head_weight.T)
    denoised = (latent - sigma_now * noise_own) / alpha_now
    step_now = math.log(alpha_next / sigma_next) - math.log(alpha_now / sigma_now)
    ratio = step_before / step_now
    blend = (1.0 + 0.5 / ratio) * denoised - 0.5 / ratio * prev_denoised
    new_latent = sigma_next / sigma_now * latent - alpha_next * (math.exp(-step_now) - 1.0) * blend
    return (hidden[None], new_latent, denoised)


def solution(mesh):
    return jax.shard_map(
        on_device,
        mesh=mesh,
        in_specs=(
            P("comp", "seq", None),
            P("comp", "seq", None),
            P("comp", "seq", None),
            P("comp", "seq"),
            P("comp", "seq"),
            P("seq", None),
        ),
        out_specs=(P("comp", "seq", None), P("comp", "seq"), P("comp", "seq")),
        check_vma=False,
    )
```

```python
import functools
import math

import jax
import jax.numpy as jnp
from jax import lax
from jax.experimental import pallas as pl
from jax.experimental.pallas import tpu as pltpu
from jax.sharding import PartitionSpec as P

HD = 128
CHUNKS = 8
WINDOW = 4
LATE = 5
MESH = pl.DeviceIdType.MESH

alpha_now = 0.6
sigma_now = 0.8
alpha_next = 0.8
sigma_next = 0.6
step_before = 0.4


def kernel(
    n, comps, own, q_hbm, k_hbm, v_hbm, w_hbm, hid_hbm, noise_ref,
    kbuf, vbuf, qbuf, obuf, wbuf, acc, sq, nsend, nrecv, relay_in, relay_mid, w_mid,
    k_send, k_recv, v_send, v_recv, q_send, q_recv, q_local,
    o_send, o_recv, o_local, w_send, w_recv, n_send, n_recv,
    in_send, in_recv, mid_send, mid_recv, back_send, piece_recv,
    wm_send, wm_recv, wb_send, w_piece,
):
    tokens, width = hid_hbm.shape
    half = width // 2
    chips = n // 2
    cw = half // CHUNKS
    rows_w = width // n
    pad = nsend.shape[2] - 8
    comp = lax.axis_index("comp")
    me = lax.axis_index("seq")
    chip, core = me // 2, me % 2
    mate = chip * 2 + 1 - core
    last = comp == comps - 1

    def peer(d_chip, d_core):
        return lax.rem(chip + d_chip, chips) * 2 + lax.rem(core + d_core, 2)

    barrier = pltpu.get_barrier_semaphore()
    others = [(dx, dc) for dx in range(chips) for dc in range(2) if (dx, dc) != (0, 0)]
    for dx, dc in others:
        pl.semaphore_signal(barrier, inc=1, device_id=(comp, peer(dx, dc)), device_id_type=MESH)

    @pl.when(jnp.logical_not(last))
    def _():
        for target in (me, mate):
            pl.semaphore_signal(
                barrier, inc=1, device_id=(comps - 1, target), device_id_type=MESH
            )
        pl.semaphore_wait(barrier, n - 1)

    @pl.when(last)
    def _():
        pl.semaphore_wait(barrier, n - 1 + 2 * (comps - 1))

    pieces, piece_rows = piece_recv.shape[0], relay_in.shape[2]
    w_pieces, piece_cols = w_piece.shape[0], w_mid.shape[2]
    helper = jnp.logical_and(jnp.logical_not(last), comp >= comps - pieces)
    w_helper = jnp.logical_and(jnp.logical_not(last), comp >= comps - w_pieces)
    final = CHUNKS - 1
    far = [(dx, dc) for dx in range(1, chips) for dc in range(2)]
    far_slots = [((chips - dx) % chips) * 2 + dc for dx, dc in far]

    def columns(side, j):
        return pl.ds(pl.multiple_of(side * half + j * cw, cw), cw)

    def kept(j):
        return pl.ds(pl.multiple_of(j * cw, cw), cw)

    def remote(src, dst, send, recv, target, owner=comp):
        return pltpu.make_async_remote_copy(
            src_ref=src, dst_ref=dst, send_sem=send, recv_sem=recv,
            device_id=(owner, target), device_id_type=MESH,
        )

    def kv_copies(dx, dc, j):
        target = peer(dx, dc)
        side = lax.rem(core + dc, 2)
        slot = ((chips - dx) % chips) * 2 + dc
        return [
            remote(src.at[0, :, columns(side, j)], buf.at[slot, :, kept(j)],
                   send.at[slot, j], recv.at[slot, j], target)
            for src, buf, send, recv in (
                (k_hbm, kbuf, k_send, k_recv), (v_hbm, vbuf, v_send, v_recv))
        ]

    def q_copy(j):
        return remote(q_hbm.at[0, :, columns(1 - core, j)], qbuf.at[1, :, kept(j)],
                      q_send.at[j], q_recv.at[j], mate)

    def local_copies(j):
        mine = columns(core, j)
        return [
            pltpu.make_async_copy(q_hbm.at[0, :, mine], qbuf.at[0, :, kept(j)], q_local.at[j]),
            pltpu.make_async_copy(k_hbm.at[0, :, mine], kbuf.at[0, :, kept(j)], k_recv.at[0, j]),
            pltpu.make_async_copy(v_hbm.at[0, :, mine], vbuf.at[0, :, kept(j)], v_recv.at[0, j]),
        ]

    def o_copies(j):
        mine = columns(core, j)
        return [
            pltpu.make_async_copy(obuf.at[0, :, kept(j)], hid_hbm.at[:, mine], o_local.at[j]),
            remote(obuf.at[1, :, kept(j)], hid_hbm.at[:, mine], o_send.at[j], o_recv.at[j], mate),
        ]

    def piece(i):
        return pl.ds(i * piece_rows, piece_rows)

    def direct_copies(dx, dc):
        slot = ((chips - dx) % chips) * 2 + dc
        side = lax.rem(core + dc, 2)
        return [
            remote(src.at[0, piece(pieces - 1), columns(side, final)],
                   buf.at[slot, piece(pieces - 1), kept(final)],
                   send.at[slot, final], piece_recv.at[pieces - 1, slot, kind], peer(dx, dc))
            for kind, (src, buf, send) in enumerate(
                ((k_hbm, kbuf, k_send), (v_hbm, vbuf, v_send)))
        ]

    def out_copies(i):
        return [
            remote(src.at[0, piece(i), columns(side, final)], relay_in.at[kind, side],
                   in_send.at[i, kind, side], in_recv.at[kind, side],
                   me, comps - pieces + i)
            for kind, src in enumerate((k_hbm, v_hbm)) for side in range(2)
        ]

    def across_copies():
        copies = []
        for (dx, dc), slot in zip(far, far_slots):
            for kind in range(2):
                copies.append(remote(
                    relay_in.at[kind, lax.rem(core + dc, 2)], relay_mid.at[slot, kind],
                    mid_send.at[slot, kind], mid_recv.at[slot, kind], peer(dx, dc)))
        return copies

    def back_copies(i):
        return [
            remote(relay_mid.at[slot, kind], buf.at[slot, piece(i), kept(final)],
                   back_send.at[slot, kind], piece_recv.at[i, slot, kind], me, comps - 1)
            for slot in far_slots for kind, buf in enumerate((kbuf, vbuf))
        ]

    def piece_arrivals(i):
        return [
            pltpu.make_async_copy(buf.at[slot, piece(i), kept(final)],
                                  buf.at[slot, piece(i), kept(final)],
                                  piece_recv.at[i, slot, kind])
            for slot in far_slots for kind, buf in enumerate((kbuf, vbuf))
        ]

    w_side = me // chips
    w_slot = lax.rem(me, chips)

    def w_cols(i):
        return pl.ds(i * piece_cols, piece_cols)

    def w_near():
        return remote(w_hbm, wbuf.at[w_slot], w_send.at[chips], w_recv.at[w_slot],
                      chip * 2 + w_side)

    def w_direct(x):
        return remote(w_hbm.at[:, w_cols(w_pieces - 1)], wbuf.at[w_slot, :, w_cols(w_pieces - 1)],
                      w_send.at[x], w_piece.at[w_pieces - 1, w_slot], x * 2 + w_side)

    def w_across(i, x):
        return remote(w_hbm.at[:, w_cols(i)], w_mid.at[w_slot],
                      wm_send.at[x], wm_recv.at[w_slot], x * 2 + w_side)

    def w_back(i, x):
        return remote(w_mid.at[x], wbuf.at[x, :, w_cols(i)],
                      wb_send.at[x], w_piece.at[i, x], me, comps - 1)

    def is_near(slot):
        return (core * chips + slot) // 2 == chip

    @pl.when(last)
    def _():
        @pl.when(chip * 2 + w_side != me)
        def _():
            w_near().start()

        @pl.when(chip * 2 + w_side == me)
        def _():
            pltpu.make_async_copy(w_hbm, wbuf.at[w_slot], w_recv.at[w_slot]).start()

        for x in range(chips):
            @pl.when(x != chip)
            def _():
                w_direct(x).start()

        acc[...] = jnp.zeros_like(acc)
        sq[...] = jnp.zeros_like(sq)

    for i in range(w_pieces - 1):
        @pl.when(comp == comps - w_pieces + i)
        def _():
            for x in range(chips):
                @pl.when(x != chip)
                def _():
                    w_across(i, x).start()

    def start_chunk(j, carry):
        cut = jnp.logical_and(last, j == final)

        def start_mate():
            for copy in kv_copies(0, 1, j):
                copy.start()
            q_copy(j).start()

        pl.when(core == 1)(start_mate)

        @pl.when(jnp.logical_not(cut))
        def _():
            for dx, dc in far:
                for copy in kv_copies(dx, dc, j):
                    copy.start()

        @pl.when(cut)
        def _():
            for dx, dc in far:
                for copy in direct_copies(dx, dc):
                    copy.start()

        pl.when(core == 0)(start_mate)
        for copy in local_copies(j):
            copy.start()
        return carry

    lax.fori_loop(0, WINDOW, start_chunk, 0)

    @pl.when(last)
    def _():
        for i in range(pieces - 1):
            for copy in out_copies(i):
                copy.start()

    def relay_across():
        @pl.when(helper)
        def _():
            for copy in out_copies(0):
                copy.wait_recv()
            for copy in across_copies():
                copy.start()

    def relay_back():
        @pl.when(helper)
        def _():
            for copy in across_copies():
                copy.wait_recv()
        for i in range(pieces - 1):
            @pl.when(comp == comps - pieces + i)
            def _():
                for copy in back_copies(i):
                    copy.start()
        for i in range(w_pieces - 1):
            @pl.when(comp == comps - w_pieces + i)
            def _():
                for x in range(chips):
                    @pl.when(jnp.logical_not(is_near(x)))
                    def _():
                        pltpu.make_async_copy(w_mid.at[x], w_mid.at[x], wm_recv.at[x]).wait()
                        w_back(i, x).start()

    def await_rows():
        for x in range(chips):
            @pl.when(is_near(x))
            def _():
                pltpu.make_async_copy(wbuf.at[x], wbuf.at[x], w_recv.at[x]).wait()

            @pl.when(jnp.logical_not(is_near(x)))
            def _():
                for i in range(w_pieces):
                    dst = wbuf.at[x, :, w_cols(i)]
                    pltpu.make_async_copy(dst, dst, w_piece.at[i, x]).wait()

    def project(j, carry):
        part = obuf[:, :, kept(j)].reshape(2 * tokens, cw)
        first = j * cw
        rows = wbuf[first // rows_w, :, pl.ds(pl.multiple_of(first % rows_w, cw), cw)]
        acc[...] += lax.dot_general(
            part, rows, (((1,), (1,)), ((), ())), preferred_element_type=jnp.float32
        )
        wide = part.astype(jnp.float32)
        sq[...] += jnp.sum(wide * wide, axis=1, keepdims=True)
        return carry

    factor = HD ** (-0.5) * math.log2(math.e)

    def attend(j, carry):
        for copy in local_copies(j):
            copy.wait()
        q_copy(j).wait_recv()
        for copy in kv_copies(0, 1, j):
            copy.wait_recv()
        cut = jnp.logical_and(last, j == final)

        @pl.when(jnp.logical_not(cut))
        def _():
            for dx, dc in far:
                for copy in kv_copies(dx, dc, j):
                    copy.wait_recv()

        @pl.when(cut)
        def _():
            for i in range(pieces):
                for copy in piece_arrivals(i):
                    copy.wait()

        pl.when(j == 1)(relay_across)
        pl.when(j == 3)(relay_back)

        @pl.when(j + WINDOW < CHUNKS)
        def _():
            start_chunk(j + WINDOW, 0)

        for h in range(cw // HD):
            cols = pl.ds(pl.multiple_of(j * cw + h * HD, HD), HD)
            query = qbuf[:, :, cols].reshape(2 * tokens, HD)
            key = kbuf[:, :, cols].reshape(n * tokens, HD)
            value = vbuf[:, :, cols].reshape(n * tokens, HD)
            scores = lax.dot_general(
                query, key, (((1,), (1,)), ((), ())), preferred_element_type=jnp.float32
            )
            highest = jnp.max(scores, axis=1, keepdims=True)
            weights = jnp.exp2((scores - highest) * factor)
            totals = jnp.sum(weights, axis=1, keepdims=True)
            out = jnp.dot(weights.astype(jnp.bfloat16), value, preferred_element_type=jnp.float32)
            out = (out / totals).astype(jnp.bfloat16)
            obuf[:, :, cols] = out.reshape(2, tokens, HD)
        for copy in o_copies(j):
            copy.start()

        @pl.when(jnp.logical_and(last, j == LATE))
        def _():
            await_rows()
            lax.fori_loop(0, LATE + 1, project, 0)

        @pl.when(jnp.logical_and(last, j > LATE))
        def _():
            project(j, 0)

        return carry

    lax.fori_loop(0, CHUNKS, attend, 0)

    def noise_copy(c, side):
        return pltpu.make_async_remote_copy(
            src_ref=nsend.at[c, side], dst_ref=nrecv.at[side],
            send_sem=n_send.at[c, side], recv_sem=n_recv.at[side],
            device_id=(c, me if side == 0 else mate), device_id_type=MESH,
        )

    def noise_self():
        return pltpu.make_async_copy(nsend.at[comps - 1, 0], nrecv.at[0], n_recv.at[0])

    @pl.when(last)
    def _():
        both = jnp.concatenate([acc[...], jnp.broadcast_to(sq[...], acc.shape)], axis=1).T
        channels = acc.shape[1]
        for c in range(comps):
            for side in range(2):
                toks = slice(side * tokens, (side + 1) * tokens)
                nsend[c, side, 0:own, :] = both[c * own:(c + 1) * own, toks]
                nsend[c, side, pad:pad + 8, :] = both[channels:channels + 8, toks]
        for c in range(comps):
            for side in range(2):
                if (c, side) == (comps - 1, 0):
                    noise_self().start()
                else:
                    noise_copy(c, side).start()

    def drain(j, carry):
        cut = jnp.logical_and(last, j == final)

        @pl.when(jnp.logical_not(cut))
        def _():
            for dx, dc in far:
                for copy in kv_copies(dx, dc, j):
                    copy.wait_send()

        @pl.when(cut)
        def _():
            for dx, dc in far:
                for copy in direct_copies(dx, dc):
                    copy.wait_send()

        for copy in kv_copies(0, 1, j):
            copy.wait_send()
        q_copy(j).wait_send()
        local, back = o_copies(j)
        local.wait()
        back.wait()
        return carry

    lax.fori_loop(0, CHUNKS, drain, 0)

    @pl.when(helper)
    def _():
        for copy in across_copies() + back_copies(0):
            copy.wait_send()

    @pl.when(w_helper)
    def _():
        for x in range(chips):
            @pl.when(x != chip)
            def _():
                w_across(0, x).wait_send()

            @pl.when(jnp.logical_not(is_near(x)))
            def _():
                w_back(0, x).wait_send()

    @pl.when(last)
    def _():
        @pl.when(chip * 2 + w_side != me)
        def _():
            w_near().wait_send()

        for x in range(chips):
            @pl.when(x != chip)
            def _():
                w_direct(x).wait_send()
        for i in range(pieces - 1):
            for copy in out_copies(i):
                copy.wait_send()
        for c in range(comps):
            for side in range(2):
                if (c, side) != (comps - 1, 0):
                    noise_copy(c, side).wait_send()

    for side in range(2):
        pltpu.make_async_copy(nsend.at[0, side], nrecv.at[side], n_recv.at[side]).wait()
    total = nrecv[0] + nrecv[1]
    root = jnp.sqrt(total[pad:pad + 1] / width + 1e-06)
    noise_ref[...] = total[0:own] / root


def on_device(queries, keys, values, latent, prev_denoised, head_weight):
    n = lax.axis_size("seq")
    comps = lax.axis_size("comp")
    _, tokens, width = queries.shape
    half = width // 2
    own = latent.shape[0]
    channels = head_weight.shape[1]
    pad = -(-own // 8) * 8
    chips, rows_w = n // 2, width // n
    pieces = min(comps, tokens // 16)
    w_pieces = min(comps, rows_w // 128)
    bf16, f32 = jnp.bfloat16, jnp.float32
    dma = pltpu.SemaphoreType.DMA
    anywhere = pl.BlockSpec(memory_space=pl.ANY)
    hidden, noise_own = pl.pallas_call(
        functools.partial(kernel, n, comps, own),
        out_shape=(
            pltpu.VMEM((tokens, width), bf16),
            pltpu.VMEM((own, tokens), f32),
        ),
        in_specs=[anywhere] * 4,
        out_specs=(anywhere, pl.BlockSpec(memory_space=pltpu.VMEM)),
        scratch_shapes=[
            pltpu.VMEM((n, tokens, half), bf16),
            pltpu.VMEM((n, tokens, half), bf16),
            pltpu.VMEM((2, tokens, half), bf16),
            pltpu.VMEM((2, tokens, half), bf16),
            pltpu.VMEM((n // 2, channels, width // n), bf16),
            pltpu.VMEM((2 * tokens, channels), f32),
            pltpu.VMEM((2 * tokens, 1), f32),
            pltpu.VMEM((comps, 2, pad + 8, tokens), f32),
            pltpu.VMEM((2, pad + 8, tokens), f32),
            pltpu.VMEM((2, 2, tokens // pieces, half // CHUNKS), bf16),
            pltpu.VMEM((n, 2, tokens // pieces, half // CHUNKS), bf16),
            pltpu.VMEM((chips, channels, rows_w // w_pieces), bf16),
            dma((n, CHUNKS)), dma((n, CHUNKS)), dma((n, CHUNKS)), dma((n, CHUNKS)),
            dma((CHUNKS,)), dma((CHUNKS,)), dma((CHUNKS,)),
            dma((CHUNKS,)), dma((CHUNKS,)), dma((CHUNKS,)),
            dma((chips + 1,)), dma((chips,)),
            dma((comps, 2)), dma((2,)),
            dma((pieces, 2, 2)), dma((2, 2)), dma((n, 2)), dma((n, 2)), dma((n, 2)),
            dma((pieces, n, 2)),
            dma((chips,)), dma((chips,)), dma((chips,)), dma((w_pieces, chips)),
        ],
        compiler_params=pltpu.CompilerParams(
            collective_id=0, has_side_effects=True, vmem_limit_bytes=60 * 1024 * 1024
        ),
        name="attention_step",
    )(queries, keys, values, head_weight.T)
    denoised = (latent - sigma_now * noise_own) / alpha_now
    step_now = math.log(alpha_next / sigma_next) - math.log(alpha_now / sigma_now)
    ratio = step_before / step_now
    blend = (1.0 + 0.5 / ratio) * denoised - 0.5 / ratio * prev_denoised
    new_latent = sigma_next / sigma_now * latent - alpha_next * (math.exp(-step_now) - 1.0) * blend
    return (hidden[None], new_latent, denoised)


def solution(mesh):
    return jax.shard_map(
        on_device,
        mesh=mesh,
        in_specs=(
            P("comp", "seq", None),
            P("comp", "seq", None),
            P("comp", "seq", None),
            P("comp", "seq"),
            P("comp", "seq"),
            P("seq", None),
        ),
        out_specs=(P("comp", "seq", None), P("comp", "seq"), P("comp", "seq")),
        check_vma=False,
    )
```
